256 devices in a mesh: dp: 16 (over x, y), head: 16 (over z, core).
Axes of the slice: x: 4, y: 4, z: 8, core: 2. Of those that a mesh axis runs over, the one named last changes fastest.
Arguments:
- student_patches: bfloat16 [16384, 256], P('dp'), may hold values from -100 to 100
- teacher_patches: bfloat16 [16384, 256], P('dp'), may hold values from -20 to 20
- mask_rows: int32 [8192], P('dp'), may hold values from 0 to 1023
- prototypes: bfloat16 [256, 131072], P(None, 'head'), may hold values from -3 to 3
Outputs:
- grad_patches: float32 [16384, 256], P('dp')
- grad_prototypes: float32 [256, 131072], P('dp', 'head')
- loss: float32 [], replicated
The draws below stay inside these ranges and needn't reach their ends.
Inputs may be any that keep to these rules, and one draw needn't show every extreme that they name: Entry i names patch row (i // 512) * 1024 + mask_rows[i]; entries may repeat.
All inputs are finite; a program needn't handle non-finite values.
Results may differ from the reference program's by a relative error of at most 0.0045.
Values sent between devices are 32-bit elements; how exact they have to be, the bound alone decides.
A program may use at most 128 MiB of HBM per device.

```python
import math
import jax
import jax.numpy as jnp
from jax import lax

B = 256
K = 131072
ROW_DEV = 512
ITERS = 3
PATCH_DEV = 1024
ROWS = 8192
PATCHES = 16384


def cluster_centres(key):
    return jnp.clip(jax.random.normal(jax.random.fold_in(key, 101), (8, B), jnp.float32), -4.0, 4.0)


def cluster_labels(key):
    block_count = PATCHES // PATCH_DEV
    dominant = jax.random.randint(jax.random.fold_in(key, 102), (block_count,), 0, 8)
    others = jax.random.randint(jax.random.fold_in(key, 103), (PATCHES,), 0, 8)
    coin = jax.random.randint(jax.random.fold_in(key, 104), (PATCHES,), 0, 10)
    block_of = jnp.arange(PATCHES, dtype=jnp.int32) // PATCH_DEV
    return jnp.where(coin < 6, jnp.take(dominant, block_of), others)


def cluster_part(key):
    return jnp.take(cluster_centres(key), cluster_labels(key), axis=0)


def block_rise(low_value, ratio):
    block_count = PATCHES // PATCH_DEV
    block_of = (jnp.arange(PATCHES, dtype=jnp.int32) // PATCH_DEV).astype(jnp.float32)
    position = block_of / max(block_count - 1, 1)
    return (low_value * ratio ** position)[:, None]


def draw_student_patches(key, part):
    shared = cluster_part(key)
    key = jax.random.fold_in(key, 3)
    key_noise, key_scale = jax.random.split(key)
    row_spread = jnp.exp(jax.random.uniform(key_scale, (PATCHES, 1), jnp.float32, math.log(0.5), math.log(5.0)))
    noise_part = jnp.clip(jax.random.normal(key_noise, (PATCHES, B), jnp.float32), -4.0, 4.0)
    strength = block_rise(0.3, 10.0)
    return ((strength * shared + noise_part) * row_spread).astype(jnp.bfloat16)


def draw_teacher_patches(key, part):
    shared = cluster_part(key)
    key = jax.random.fold_in(key, 5)
    key_noise, key_scale = jax.random.split(key)
    row_spread = jax.random.uniform(key_scale, (PATCHES, 1), jnp.float32, 0.5, 2.0)
    noise_part = jnp.clip(jax.random.normal(key_noise, (PATCHES, B), jnp.float32), -4.0, 4.0)
    strength = 1.5
    return ((strength * shared + noise_part) * row_spread).astype(jnp.bfloat16)


def draw_prototypes(key, part):
    centres = cluster_centres(key)
    key = jax.random.fold_in(key, 7)
    key_noise, key_scale, key_region, key_pick, key_factor = jax.random.split(key, 5)
    col_spread = jnp.exp(jax.random.uniform(key_scale, (1, K), jnp.float32, math.log(0.3), math.log(3.0)))
    region_width = K // 16
    region_strength = 2.0 * jax.random.uniform(key_region, (16,), jnp.float32) ** 2
    region_cluster = jax.random.randint(key_pick, (16,), 0, 8)
    col_region = jnp.arange(K, dtype=jnp.int32) // region_width
    col_factor = jax.random.uniform(key_factor, (K,), jnp.float32, 0.5, 1.0)
    col_strength = jnp.take(region_strength, col_region) * col_factor
    aligned = jnp.take(jnp.take(centres, region_cluster, axis=0).T, col_region, axis=1)
    noise_part = jnp.clip(jax.random.normal(key_noise, (B, K), jnp.float32), -4.0, 4.0)
    mixed = noise_part + col_strength[None, :] * aligned
    return (mixed * col_spread / math.sqrt(B)).astype(jnp.bfloat16)


def place_ends(values, own_key, least, high):
    longest = values.shape.index(max(values.shape))
    spots = []
    for shift in (0, 1):
        where = [jax.random.randint(jax.random.fold_in(own_key, axis), (), 0, length) for axis, length in enumerate(values.shape)]
        where[longest] = (where[longest] + shift) % values.shape[longest]
        spots.append(tuple(where))
    return values.at[spots[0]].set(least).at[spots[1]].set(high)


def setup_inputs(seed: int = 0) -> dict:
    key_list = jax.random.split(jax.random.key(seed), 5)
    student_patches = draw_student_patches(jax.random.fold_in(key_list[4], 71), 0)
    teacher_patches = draw_teacher_patches(jax.random.fold_in(key_list[4], 71), 0)
    mask_rows = place_ends(jax.random.randint(key_list[2], (ROWS,), 0, PATCH_DEV), jax.random.fold_in(key_list[2], 1), 0, PATCH_DEV - 1).astype(jnp.int32)
    prototypes = draw_prototypes(jax.random.fold_in(key_list[4], 71), 0)
    return dict(student_patches=student_patches, teacher_patches=teacher_patches, mask_rows=mask_rows, prototypes=prototypes)


eps = 1e-06
teacher_temp = 0.04
student_temp = 0.1
loss_scale = 4096.0
highest = lax.Precision.HIGHEST

def unit_rows(values):
    inverse = lax.rsqrt(lax.optimization_barrier(jnp.sum(values * values, axis=1, keepdims=True)) + eps)
    return (values * inverse, inverse)

def reference(student_patches, teacher_patches, mask_rows, prototypes):
    offsets = jnp.arange(ROWS, dtype=jnp.int32) // ROW_DEV * PATCH_DEV
    picked = (mask_rows + offsets).astype(jnp.int32)
    student_unit, inv_norm = unit_rows(jnp.take(student_patches, picked, axis=0).astype(jnp.float32))
    student_unit = student_unit.astype(jnp.bfloat16)
    teacher_unit = unit_rows(jnp.take(teacher_patches, picked, axis=0).astype(jnp.float32))[0].astype(jnp.bfloat16)
    weight = prototypes.astype(jnp.float32)
    col_inv = lax.rsqrt(lax.optimization_barrier(jnp.sum(weight * weight, axis=0)) + eps)
    normed = (weight * col_inv[None, :]).astype(jnp.bfloat16)
    block_cols = min(8192, K)
    num_blocks = K // block_cols
    proto_blocks = jnp.transpose(normed.reshape(B, num_blocks, block_cols), (1, 0, 2))

    def teacher_exp(proto_block):
        return jnp.exp(jnp.dot(teacher_unit, proto_block, preferred_element_type=jnp.float32) / teacher_temp)

    def student_raw(proto_block):
        return jnp.dot(student_unit, proto_block, preferred_element_type=jnp.float32)
    sample_scale = jnp.ones((ROWS,), jnp.float32)
    proto_scale = jnp.ones((num_blocks, block_cols), jnp.float32)
    for sweep in range(ITERS):

        def col_pass(proto_block):
            return 1.0 / (K * jnp.dot(sample_scale, teacher_exp(proto_block), precision=highest))
        proto_scale = lax.map(col_pass, proto_blocks)

        def row_pass(summed, inputs):
            proto_block, col_scale = inputs
            return (summed + jnp.dot(teacher_exp(proto_block), col_scale, precision=highest), None)
        row_total, _ = lax.scan(row_pass, jnp.zeros((ROWS,), jnp.float32), (proto_blocks, proto_scale))
        sample_scale = 1.0 / (ROWS * row_total)

    def exp_pass(summed, proto_block):
        return (summed + lax.optimization_barrier(jnp.sum(jnp.exp(student_raw(proto_block) / student_temp), axis=1)), None)
    exp_total, _ = lax.scan(exp_pass, jnp.zeros((ROWS,), jnp.float32), proto_blocks)
    log_total = jnp.log(exp_total)

    def grad_pass(totals, inputs):
        unit_grad, loss_sum = totals
        proto_block, col_scale = inputs
        target = ROWS * sample_scale[:, None] * teacher_exp(proto_block) * col_scale[None, :]
        log_prob = student_raw(proto_block) / student_temp - log_total[:, None]
        loss_sum = loss_sum + jnp.sum(target * log_prob)
        grads = (loss_scale * (jnp.exp(log_prob) - target) / student_temp).astype(jnp.bfloat16)
        unit_grad = unit_grad + jnp.dot(grads, proto_block.T, preferred_element_type=jnp.float32)
        normed_grad = jnp.dot(student_unit.T, grads, preferred_element_type=jnp.float32)
        block_float = proto_block.astype(jnp.float32)
        col_dot = lax.optimization_barrier(jnp.sum(block_float * normed_grad, axis=0))
        return ((unit_grad, loss_sum), normed_grad - block_float * col_dot[None, :])
    start_totals = (jnp.zeros((ROWS, B), jnp.float32), jnp.zeros((), jnp.float32))
    (unit_grad, loss_sum), corrected = lax.scan(grad_pass, start_totals, (proto_blocks, proto_scale))
    grad_prototypes = col_inv[None, :] * jnp.transpose(corrected, (1, 0, 2)).reshape(B, K)
    unit_float = student_unit.astype(jnp.float32)
    row_dot = lax.optimization_barrier(jnp.sum(unit_float * unit_grad, axis=1, keepdims=True))
    d_rows = inv_norm * (unit_grad - unit_float * row_dot)
    grad_patches = jnp.zeros((PATCHES, B), jnp.float32).at[picked].add(d_rows)
    loss = -loss_sum / ROWS
    return (grad_patches, grad_prototypes, loss)
```

```python
import functools
import math

import jax
import jax.numpy as jnp
from jax import lax
from jax.experimental import pallas as pl
from jax.experimental.pallas import tpu as pltpu
from jax.sharding import PartitionSpec as P

MESH = pl.DeviceIdType.MESH
F32, BF16 = jnp.float32, jnp.bfloat16

EPS = 1e-06
LOG2E = math.log2(math.e)
TEACHER = 25.0 * LOG2E
STUDENT = 10.0 * LOG2E
GRAD = 4096.0 / 0.1
ITERS = 3
DP, HEAD, SIDE, DEEP = 16, 16, 4, 8
R, B, C = 512, 256, 8192
W = C // DP
ROWS, K = R * DP, C * HEAD
S = R // HEAD

X0, Y0, H0 = 0, 3, 6
INV, SS, CU, ZU, CP, ZP, AGZ, AGC, A2A, LD, LH = range(9, 20)
SMALL = 20

A1, F1 = lambda u, s: u * 2 + s, lambda u, s: 4 + u * 2 + s
A2, F2 = lambda u, m, s: 8 + (u * 4 + m) * 2 + s, lambda u, m, s: 24 + (u * 4 + m) * 2 + s
MATE = lambda a, b: 40 + a * 4 + b
GATHER = 56
SHIFT = (0, 3, 1, 2)


def nt(a, b):
    return lax.dot_general(a, b, (((1,), (1,)), ((), ())), preferred_element_type=F32)


def nn(a, b):
    return jnp.dot(a, b, preferred_element_type=F32)


def kernel(student, teacher, mask, proto, patch_out, proto_out, loss_out,
           oh, su, tu, invn, nrm, nown, colinv, E, G, ET, suT, PG, TG,
           U, PU, cr, zs, zr, csum, ysum, xr, yr, cs, racc, eacc, sscol,
           hsrc, hr, iva, ssa, agb, a2s, a2r, dhi, dlo, ldr, lhr,
           psend, precv, gsend, grecv, lsem):
    i, j = lax.axis_index("dp"), lax.axis_index("head")
    x, y = i // SIDE, lax.rem(i, SIDE)
    z, c = j // 2, lax.rem(j, 2)
    mate = (i, z * 2 + 1 - c)

    QUARTER = C // 4

    def proto_copy(k):
        cols = pl.ds(k * QUARTER, QUARTER)
        return pltpu.make_async_copy(proto.at[:, cols], nrm.at[:, cols], lsem.at[k])

    for k in range(4):
        proto_copy(k).start()

    barrier = pltpu.get_barrier_semaphore()
    for d in range(1, DP):
        pl.semaphore_signal(barrier, inc=1, device_id=(lax.rem(i + d, DP), j), device_id_type=MESH)
        pl.semaphore_signal(barrier, inc=1, device_id=(i, lax.rem(j + d, HEAD)), device_id_type=MESH)

    def send(src, dst, ph, dev):
        pltpu.make_async_remote_copy(src, dst, psend.at[ph], precv.at[ph], device_id=dev, device_id_type=MESH).start()

    def landed(like, ph):
        pltpu.make_async_copy(like, like, precv.at[ph]).wait()

    def sent(like, ph):
        pltpu.make_async_copy(like, like, psend.at[ph]).wait()

    def along_x(d):
        return (lax.rem(x + d, SIDE) * SIDE + y, j)

    def along_y(d):
        return (x * SIDE + lax.rem(y + d, SIDE), j)

    def along_dp(d):
        return (lax.rem(i + d, DP), j)

    def along_head(d):
        return (i, lax.rem(j + d, HEAD))

    def along_z(d):
        return (i, lax.rem(z + d, DEEP) * 2 + c)

    p = x * (1 - c) + y * c
    q = y * (1 - c) + x * c

    def at(dp_, dq_):
        pp, qq = lax.rem(p + dp_, SIDE), lax.rem(q + dq_, SIDE)
        return (pp * SIDE + qq) * (1 - c) + (qq * SIDE + pp) * c

    HALF = R // 4

    def part(blk, u, half=None):
        if half is None:
            return G.at[blk, c, u]
        return G.at[blk, c, u, pl.ds(half * HALF, HALF)]

    def gcopy(ref, sid, dev):
        return pltpu.make_async_remote_copy(ref, ref, gsend.at[sid], grecv.at[sid], device_id=dev, device_id_type=MESH)

    def gwait(ref, sid):
        pltpu.make_async_copy(ref, ref, grecv.at[sid]).wait()

    def n1(s):
        return (at(1 if s == 0 else 3, 0), j)

    def n2(s):
        return (at(0, 1 if s == 0 else 3), j)

    def a1_send(u):
        for s in (0, 1):
            gcopy(part(at(0, 0), u), A1(u, s), n1(s)).start()

    def a1_wait(u):
        for s in (0, 1):
            gwait(part(at(3 if s == 0 else 1, 0), u), A1(u, s))

    def f1_send(u):
        for s in (0, 1):
            gcopy(part(at(3 if s == 0 else 1, 0), u, s), F1(u, s), n1(s)).start()

    def f1_wait(u):
        for s in (0, 1):
            gwait(part(at(2, 0), u, s), F1(u, s))

    def a2_send(u, m):
        for s in (0, 1):
            gcopy(part(at(SHIFT[m], 0), u), A2(u, m, s), n2(s)).start()

    def a2_wait(u, m):
        for s in (0, 1):
            gwait(part(at(SHIFT[m], 3 if s == 0 else 1), u), A2(u, m, s))

    def f2_send(u, m):
        for s in (0, 1):
            gcopy(part(at(SHIFT[m], 3 if s == 0 else 1), u, s), F2(u, m, s), n2(s)).start()

    def f2_wait(u, m):
        for s in (0, 1):
            gwait(part(at(SHIFT[m], 2), u, s), F2(u, m, s))

    def mate_send(a, b):
        ref = G.at[at(a, b), c]
        pltpu.make_async_remote_copy(ref, ref, gsend.at[MATE(a, b)], grecv.at[MATE(a, b)], device_id=mate, device_id_type=MESH).start()

    def mate_wait(a, b):
        ref = G.at[at(a, b), 1 - c]
        pltpu.make_async_copy(ref, ref, grecv.at[MATE(b, a)]).wait()

    def slot(n):
        if n == 0:
            a1_send(0)
            a2_send(0, 0)
        elif n == 1:
            a1_send(1)
            a2_send(1, 0)
        elif n in (2, 3):
            u = n - 2
            a1_wait(u)
            f1_send(u)
            a2_wait(u, 0)
            f2_send(u, 0)
            a2_send(u, 1)
            if u == 1:
                for a, b in ((1, 0), (3, 0), (0, 1), (0, 3)):
                    mate_send(a, b)
        elif n in (4, 5):
            u = n - 4
            a2_wait(u, 1)
            f2_send(u, 1)
            a2_send(u, 2)
            f1_wait(u)
            f2_wait(u, 0)
            if u == 1:
                for a, b in ((2, 0), (0, 2), (3, 1), (3, 3)):
                    mate_send(a, b)
        elif n in (6, 7):
            u = n - 6
            a2_wait(u, 2)
            f2_send(u, 2)
            a2_send(u, 3)
            f2_wait(u, 1)
            if u == 1:
                for a, b in ((3, 2), (1, 1), (1, 3)):
                    mate_send(a, b)
        elif n == 8:
            a2_wait(0, 3)
            f2_send(0, 3)
            a2_wait(1, 3)
            f2_send(1, 3)
            f2_wait(0, 2)
            f2_wait(1, 2)
            for a, b in ((2, 1), (2, 3), (1, 2)):
                mate_send(a, b)
        elif n == 9:
            f2_wait(0, 3)
            f2_wait(1, 3)
            mate_send(2, 2)

    @pl.loop(0, 8)
    def _(k):
        rows = pl.ds(pl.multiple_of(k * 128, 128), 128)
        patch = lax.broadcasted_iota(jnp.int32, (128, R), 0) + k * 128
        oh[rows, :] = jnp.where(patch == mask[...], 1.0, 0.0).astype(BF16)

    def unit(patches):
        rows = lax.dot_general(oh[...], patches[...], (((0,), (0,)), ((), ())), preferred_element_type=F32)
        inverse = lax.rsqrt(jnp.sum(rows * rows, axis=1, keepdims=True) + EPS)
        return (rows * inverse).astype(BF16), inverse

    unit_s, inv_s = unit(student)
    su[...] = unit_s
    invn[...] = jnp.broadcast_to(inv_s, (R, 128))
    unit_t, _ = unit(teacher)
    tu[...] = unit_t
    for half in (0, 1):
        rows = slice(half * (R // 2), (half + 1) * (R // 2))
        G[i, half, 0] = su[rows, :].astype(F32)
        G[i, half, 1] = tu[rows, :].astype(F32)

    pl.semaphore_wait(barrier, DP + HEAD - 2)
    slot(0)

    for k in range(4):
        proto_copy(k).wait()

    @pl.loop(0, C // W)
    def _(k):
        cols = pl.ds(pl.multiple_of(k * W, W), W)
        w = nrm[:, cols].astype(F32)
        inverse = lax.rsqrt(jnp.sum(w * w, axis=0, keepdims=True) + EPS)
        n = (w * inverse).astype(BF16)
        colinv[:, cols] = inverse
        nrm[:, cols] = n
        e = jnp.exp2(nn(tu[...], n) * TEACHER)
        E[:, cols] = e
        csum[0, :, cols] = jnp.sum(e, axis=0, keepdims=True)

    mine = pl.ds(pl.multiple_of(i * W, W), W)
    nown[...] = nrm[:, mine]
    PU[...] = jnp.zeros_like(PU)
    U[...] = jnp.zeros_like(U)
    PG[...] = jnp.zeros_like(PG)
    TG[...] = jnp.zeros_like(TG)
    eacc[...] = jnp.zeros_like(eacc)

    def tiles(v):
        total = v[:, 0:128]
        for t in range(1, v.shape[1] // 128):
            total = total + v[:, t * 128:(t + 1) * 128]
        return total

    def student_chunks(first, last):
        @pl.loop(first, last)
        def _(k):
            cols = pl.ds(pl.multiple_of(k * W, W), W)
            n = nrm[:, cols]
            e = jnp.exp2(nn(su[...], n) * STUDENT)
            eacc[...] += tiles(e)
            PU[...] += nt(e.astype(BF16), n).reshape(DEEP, 2, S, B)

    def across(v):
        return jnp.sum(v.T, axis=0, keepdims=True)

    def down(v):
        return jnp.broadcast_to(v, (128, R)).T

    def row_pass():
        @pl.loop(0, R // 64)
        def _(k):
            rows = pl.ds(pl.multiple_of(k * 64, 64), 64)
            total = jnp.zeros((64, 128), F32)
            for t in range(C // 128):
                total = total + E[rows, t * 128:(t + 1) * 128] * cs[:, t * 128:(t + 1) * 128]
            racc[rows, :] = total

    def last_row_pass():
        racc[...] = jnp.zeros_like(racc)

        @pl.loop(0, C // W)
        def _(k):
            cols = pl.ds(pl.multiple_of(k * W, W), W)
            t = E[:, cols] * cs[:, cols]
            racc[...] += tiles(t)
            U[...] += nt(t.astype(BF16), nrm[:, cols]).reshape(DEEP, 2, S, B)

    def col_pass(it):
        @pl.loop(0, C // 1024)
        def _(k):
            cols = pl.ds(pl.multiple_of(k * 1024, 1024), 1024)
            total = jnp.zeros((8, 1024), F32)
            for r in range(R // 8):
                scale = sscol[r * 8:(r + 1) * 8, :]
                total = total + E[r * 8:(r + 1) * 8, cols] * jnp.concatenate([scale] * 8, axis=1)
            csum[it, :, cols] = jnp.sum(total, axis=0, keepdims=True)

    def block(a, b):
        blk = at(a, b)
        s = G[blk, :, 0].reshape(R, B).astype(BF16)
        t = G[blk, :, 1].reshape(R, B).astype(BF16)
        ET[blk] = jnp.exp2(nn(t, nown[...]) * TEACHER).astype(BF16)
        e = jnp.exp2(nn(s, nown[...]) * STUDENT).astype(BF16)
        turned = s.astype(F32).T
        suT[blk] = turned.astype(BF16)
        PG[...] += nn((turned * iva[blk]).astype(BF16), e)

    def blocks(pairs):
        for a, b in pairs:
            if (a, b) != (0, 0):
                mate_wait(a, b)
            block(a, b)

    def core_sum_send(v, which, ph):
        send(v.at[:, 1 - c], cr.at[which], ph, mate)

    def core_sum_wait(v, which, ph, zph):
        landed(cr.at[which], ph)
        zs[which] = v[:, c] + cr[which]
        for d in range(1, DEEP):
            send(zs.at[which, lax.rem(z + d, DEEP)], zr.at[which, d - 1], zph, along_z(d))

    def z_sum(which, zph):
        landed(zr.at[which], zph)
        total = zs[which, z]
        for d in range(DEEP - 1):
            total = total + zr[which, d]
        return total

    for it in range(ITERS):
        for d in range(1, SIDE):
            send(csum.at[it], xr.at[it, d - 1], X0 + it, along_x(d))
        slot(3 * it + 1)
        if it == 0:
            student_chunks(0, 5)
        elif it == 1:
            landed(iva.at[pl.ds(0, DP - 1)], INV)
            blocks(((0, 0),))
            core_sum_wait(PU, 0, CP, ZP)
        elif it == 2:
            blocks(((0, 2), (3, 1), (3, 3)))
        landed(xr.at[it], X0 + it)
        ysum[it] = csum[it] + xr[it, 0] + xr[it, 1] + xr[it, 2]
        for d in range(1, SIDE):
            send(ysum.at[it], yr.at[it, d - 1], Y0 + it, along_y(d))
        slot(3 * it + 2)
        if it == 0:
            student_chunks(5, 16)
        elif it == 1:
            blocks(((1, 0), (3, 0), (0, 1)))
        elif it == 2:
            blocks(((3, 2), (1, 1), (1, 3)))
        landed(yr.at[it], Y0 + it)
        cs[...] = 1.0 / (K * (ysum[it] + yr[it, 0] + yr[it, 1] + yr[it, 2]))
        if it < ITERS - 1:
            row_pass()
        else:
            last_row_pass()
            core_sum_send(U, 1, CU)
        hsrc[it, :, 0:R] = across(racc[...])
        if it == 0:
            hsrc[it, :, R:2 * R] = across(eacc[...])
        wide = 2 * R if it == 0 else R
        for d in range(1, HEAD):
            send(hsrc.at[it, :, pl.ds(0, wide)], hr.at[it, d - 1, :, pl.ds(0, wide)], H0 + it, along_head(d))
        slot(3 * it + 3)
        if it == 0:
            core_sum_send(PU, 0, CP)
        elif it == 1:
            blocks(((0, 3), (2, 0)))
        elif it == 2:
            core_sum_wait(U, 1, CU, ZU)
        landed(hr.at[it, :, :, pl.ds(0, wide)], H0 + it)
        row_total = hsrc[it, :, 0:R]
        for d in range(HEAD - 1):
            row_total = row_total + hr[it, d, :, 0:R]
        if it == 0:
            exp_total = hsrc[it, :, R:2 * R]
            for d in range(HEAD - 1):
                exp_total = exp_total + hr[it, d, :, R:2 * R]
            iva[i] = 1.0 / exp_total
            for d in range(1, DP):
                send(iva.at[i], iva.at[i], INV, along_dp(d))
        if it < ITERS - 1:
            sscol[...] = down(1.0 / (ROWS * row_total))
            col_pass(it + 1)

    ssa[i] = 1.0 / row_total
    for d in range(1, DP):
        send(ssa.at[i], ssa.at[i], SS, along_dp(d))
    blocks(((2, 1), (2, 3), (1, 2), (2, 2)))
    landed(ssa.at[pl.ds(0, DP - 1)], SS)

    @pl.loop(0, DP)
    def _(k):
        TG[...] += nn((suT[k].astype(F32) * ssa[k]).astype(BF16), ET[k])

    unit_cols = nown[...].astype(F32)
    normed_grad = GRAD * (PG[...] - cs[:, mine] * TG[...])
    col_dot = jnp.sum(unit_cols * normed_grad, axis=0, keepdims=True)
    a2s[...] = (colinv[:, mine] * (normed_grad - unit_cols * col_dot)).reshape(DP, B // DP, W)
    for d in range(1, DP):
        send(a2s.at[lax.rem(i + d, DP)], a2r.at[i], A2A, along_dp(d))
    a2r[i] = a2s[i]

    target_sum = z_sum(1, ZU)
    student_sum = z_sum(0, ZP)
    own = lax.broadcasted_iota(jnp.int32, (S, R), 1) == lax.broadcasted_iota(jnp.int32, (S, R), 0) + j * S

    def pick(v):
        return jnp.sum(jnp.where(own, v, 0.0), axis=1, keepdims=True)

    own_rows = pl.ds(pl.multiple_of(j * S, S), S)
    in_half = pl.ds(pl.multiple_of(lax.rem(j, 8) * S, S), S)
    unit_rows = G[i, j // 8, 0, in_half]
    target_mean = target_sum * pick(ssa[i])
    exp_inv = pick(iva[i])
    unit_grad = GRAD * (student_sum * exp_inv - target_mean)
    row_dot = jnp.sum(unit_rows * unit_grad, axis=1, keepdims=True)
    agb[c, z] = invn[own_rows, 0:1] * (unit_grad - unit_rows * row_dot)
    for d in range(1, DEEP):
        send(agb.at[c, z], agb.at[c, z], AGZ, along_z(d))
    raw_mean = jnp.sum(unit_rows * target_mean, axis=1, keepdims=True)
    part_loss = jnp.sum(raw_mean * 10.0 + jnp.log(exp_inv), axis=0, keepdims=True)
    ldr[i] = jnp.broadcast_to(part_loss, (1, 128))
    for d in range(1, DP):
        send(ldr.at[i], ldr.at[i], LD, along_dp(d))

    landed(agb.at[c, pl.ds(0, DEEP - 1)], AGZ)
    send(agb.at[c], agb.at[c], AGC, mate)
    landed(a2r.at[pl.ds(0, DP - 1)], A2A)
    for d in range(DP):
        proto_out[:, d * W:(d + 1) * W] = a2r[d]
    landed(ldr.at[pl.ds(0, DP - 1)], LD)
    total = ldr[0]
    for d in range(1, DP):
        total = total + ldr[d]
    lhr[j] = total
    for d in range(1, HEAD):
        send(lhr.at[j], lhr.at[j], LH, along_head(d))

    landed(agb.at[1 - c], AGC)
    for k in range(DEEP):
        for h in (0, 1):
            rows = slice((k * 2 + h) * S, (k * 2 + h + 1) * S)
            v = agb[h, k]
            high = v.astype(BF16)
            dhi[rows, :] = high
            dlo[rows, :] = (v - high.astype(F32)).astype(BF16)

    @pl.loop(0, 4)
    def _(k):
        rows = pl.ds(pl.multiple_of(k * 256, 256), 256)
        patch_out[rows, :] = nn(oh[rows, :], dhi[...]) + nn(oh[rows, :], dlo[...])

    landed(lhr.at[pl.ds(0, HEAD - 1)], LH)
    total = lhr[0]
    for d in range(1, HEAD):
        total = total + lhr[d]
    loss_out[...] = total * (-1.0 / ROWS)

    for it in range(ITERS):
        sent(xr.at[it], X0 + it)
        sent(yr.at[it], Y0 + it)
        wide = 2 * R if it == 0 else R
        sent(hr.at[it, :, :, pl.ds(0, wide)], H0 + it)
    sent(iva.at[pl.ds(0, DP - 1)], INV)
    sent(ssa.at[pl.ds(0, DP - 1)], SS)
    sent(cr.at[1], CU)
    sent(cr.at[0], CP)
    sent(zr.at[1], ZU)
    sent(zr.at[0], ZP)
    sent(agb.at[c, pl.ds(0, DEEP - 1)], AGZ)
    sent(agb.at[c], AGC)
    sent(a2r.at[pl.ds(0, DP - 1)], A2A)
    sent(ldr.at[pl.ds(0, DP - 1)], LD)
    sent(lhr.at[pl.ds(0, HEAD - 1)], LH)
    whole, half = part(i, 0), part(i, 0, 0)

    def gsent(like, sid):
        pltpu.make_async_copy(like, like, gsend.at[sid]).wait()

    for u in (0, 1):
        for s in (0, 1):
            gsent(whole, A1(u, s))
            gsent(half, F1(u, s))
            for m in range(4):
                gsent(whole, A2(u, m, s))
                gsent(half, F2(u, m, s))
    for a in range(SIDE):
        for b in range(SIDE):
            if (a, b) != (0, 0):
                gsent(G.at[i, c], MATE(a, b))


def on_device(student_patches, teacher_patches, mask_rows, prototypes):
    vm = pltpu.VMEM
    whole = pl.BlockSpec(memory_space=pltpu.VMEM)
    patches, protos, loss = pl.pallas_call(
        kernel,
        out_shape=(
            jax.ShapeDtypeStruct(student_patches.shape, F32),
            jax.ShapeDtypeStruct((B // DP, C), F32),
            jax.ShapeDtypeStruct((1, 128), F32),
        ),
        in_specs=[whole] * 3 + [pl.BlockSpec(memory_space=pl.ANY)],
        out_specs=(whole, whole, whole),
        scratch_shapes=[
            vm((1024, R), BF16),
            vm((R, B), BF16),
            vm((R, B), BF16),
            vm((R, 128), F32),
            vm((B, C), BF16),
            vm((B, W), BF16),
            vm((1, C), F32),
            vm((R, C), F32),
            vm((DP, 2, 2, R // 2, B), F32),
            vm((DP, R, W), BF16),
            vm((DP, B, R), BF16),
            vm((B, W), F32),
            vm((B, W), F32),
            vm((DEEP, 2, S, B), F32),
            vm((DEEP, 2, S, B), F32),
            vm((2, DEEP, S, B), F32),
            vm((2, DEEP, S, B), F32),
            vm((2, DEEP - 1, S, B), F32),
            vm((ITERS, 1, C), F32),
            vm((ITERS, 1, C), F32),
            vm((ITERS, SIDE - 1, 1, C), F32),
            vm((ITERS, SIDE - 1, 1, C), F32),
            vm((1, C), F32),
            vm((R, 128), F32),
            vm((R, 128), F32),
            vm((R, 128), F32),
            vm((ITERS, 1, 2 * R), F32),
            vm((ITERS, HEAD - 1, 1, 2 * R), F32),
            vm((DP, 1, R), F32),
            vm((DP, 1, R), F32),
            vm((2, DEEP, S, B), F32),
            vm((DP, B // DP, W), F32),
            vm((DP, B // DP, W), F32),
            vm((R, B), BF16),
            vm((R, B), BF16),
            vm((DP, 1, 128), F32),
            vm((HEAD, 1, 128), F32),
            pltpu.SemaphoreType.DMA((SMALL,)),
            pltpu.SemaphoreType.DMA((SMALL,)),
            pltpu.SemaphoreType.DMA((GATHER,)),
            pltpu.SemaphoreType.DMA((GATHER,)),
            pltpu.SemaphoreType.DMA((4,)),
        ],
        compiler_params=pltpu.CompilerParams(
            collective_id=0, has_side_effects=True, vmem_limit_bytes=63 * 2**20
        ),
    )(student_patches, teacher_patches, mask_rows.reshape(1, R), prototypes)
    return patches, protos, loss[0, 0]


def solution(mesh):
    return jax.shard_map(
        on_device,
        mesh=mesh,
        in_specs=(P("dp", None), P("dp", None), P("dp"), P(None, "head")),
        out_specs=(P("dp", None), P("dp", "head"), P()),
        check_vma=False,
    )
```

```python
import functools
import math

import jax
import jax.numpy as jnp
from jax import lax
from jax.experimental import pallas as pl
from jax.experimental.pallas import tpu as pltpu
from jax.sharding import PartitionSpec as P

MESH = pl.DeviceIdType.MESH
F32, BF16 = jnp.float32, jnp.bfloat16

EPS = 1e-06
LOG2E = math.log2(math.e)
TEACHER = 25.0 * LOG2E
STUDENT = 10.0 * LOG2E
GRAD = 4096.0 / 0.1
ITERS = 3
DP, HEAD, SIDE, DEEP = 16, 16, 4, 8
R, B, C = 512, 256, 8192
W = C // DP
ROWS, K = R * DP, C * HEAD
S = R // HEAD

CH = 4
CW = C // CH
LAST_W = 1024
X0, Y0, H0 = 0, ITERS * CH, 2 * ITERS * CH
INV, SS, CU, ZU, CP, ZP, AGZ, AGC, LD, LH, A2A = range(H0 + ITERS, H0 + ITERS + 11)
SMALL = A2A + 2


def far_first(sides):
    offsets = [(a, b) for a in range(sides[0]) for b in range(sides[1]) if (a, b) != (0, 0)]
    return sorted(offsets, key=lambda o: -min(o[0], sides[0] - o[0]) - min(o[1], sides[1] - o[1]))


DP_OFF, HEAD_OFF = far_first((SIDE, SIDE)), far_first((DEEP, 2))

A1, F1 = lambda u, s: u * 2 + s, lambda u, s: 4 + u * 2 + s
A2, F2 = lambda u, m, s: 8 + (u * 4 + m) * 2 + s, lambda u, m, s: 24 + (u * 4 + m) * 2 + s
MATE = lambda a, b: 40 + a * 4 + b
ZED = lambda a, b, s: 56 + (a * 4 + b) * 2 + s
GATHER = 88
PLANE, BESIDE = 176, 80
SHIFT = (0, 3, 1, 2)


def nt(a, b):
    return lax.dot_general(a, b, (((1,), (1,)), ((), ())), preferred_element_type=F32)


def nn(a, b):
    return jnp.dot(a, b, preferred_element_type=F32)


def kernel(student, teacher, mask, proto, patch_out, proto_out, loss_out,
           oh, su, tu, invn, nrm, nown, colinv, E, G, ET, suT, PG,
           U, PU, cr, zs, zr, csum, ysum, xr, yr, cs, racc, eacc, sscol,
           hsrc, hr, iva, ssa, agb, a2s, a2r, wide_out, dhi, dlo, ldr, lhr,
           psend, precv, gsend, grecv, lsem, osem):
    i, j = lax.axis_index("dp"), lax.axis_index("head")
    x, y = i // SIDE, lax.rem(i, SIDE)
    z, c = j // 2, lax.rem(j, 2)
    mate = (i, z * 2 + 1 - c)

    def proto_copy(k):
        cols = pl.ds(k * CW, CW)
        return pltpu.make_async_copy(proto.at[:, cols], nrm.at[:, cols], lsem.at[k])

    for k in range(CH):
        proto_copy(k).start()

    barrier = pltpu.get_barrier_semaphore()
    for d in range(1, DP):
        pl.semaphore_signal(barrier, inc=1, device_id=(lax.rem(i + d, DP), j), device_id_type=MESH)
        pl.semaphore_signal(barrier, inc=1, device_id=(i, lax.rem(j + d, HEAD)), device_id_type=MESH)

    def send(src, dst, ph, dev):
        pltpu.make_async_remote_copy(src, dst, psend.at[ph], precv.at[ph], device_id=dev, device_id_type=MESH).start()

    def landed(like, ph):
        pltpu.make_async_copy(like, like, precv.at[ph]).wait()

    def sent(like, ph):
        pltpu.make_async_copy(like, like, psend.at[ph]).wait()

    def along_x(d):
        return (lax.rem(x + d, SIDE) * SIDE + y, j)

    def along_y(d):
        return (x * SIDE + lax.rem(y + d, SIDE), j)

    def to_dp(src, dst, ph):
        for a, b in DP_OFF:
            send(src, dst, ph, (lax.rem(x + a, SIDE) * SIDE + lax.rem(y + b, SIDE), j))

    def to_head(src, dst, ph):
        for e, (a, b) in enumerate(HEAD_OFF):
            send(src, dst(e), ph, (i, lax.rem(z + a, DEEP) * 2 + lax.rem(c + b, 2)))

    def along_z(d):
        return (i, lax.rem(z + d, DEEP) * 2 + c)

    p = x * (1 - c) + y * c
    q = y * (1 - c) + x * c

    def at(dp_, dq_):
        pp, qq = lax.rem(p + dp_, SIDE), lax.rem(q + dq_, SIDE)
        return (pp * SIDE + qq) * (1 - c) + (qq * SIDE + pp) * c

    odd = lax.rem(z, 2)

    def part(blk, u, half=None):
        first = odd * BESIDE + (0 if half is None else half * (PLANE // 2))
        rows = pl.ds(pl.multiple_of(first, 8), PLANE if half is None else PLANE // 2)
        return G.at[blk, c, u, rows]

    def beside(blk, which, s):
        first = which * PLANE + s * (BESIDE // 2)
        return G.at[blk, c, :, pl.ds(pl.multiple_of(first, 8), BESIDE // 2)]

    def z_send(pairs):
        for a, b in pairs:
            for s in (0, 1):
                gcopy(beside(at(a, b), odd, s), ZED(a, b, s), along_z(1 if s == 0 else DEEP - 1)).start()

    def gcopy(ref, sid, dev):
        return pltpu.make_async_remote_copy(ref, ref, gsend.at[sid], grecv.at[sid], device_id=dev, device_id_type=MESH)

    def gwait(ref, sid):
        pltpu.make_async_copy(ref, ref, grecv.at[sid]).wait()

    def n1(s):
        return (at(1 if s == 0 else 3, 0), j)

    def n2(s):
        return (at(0, 1 if s == 0 else 3), j)

    def a1_send(u):
        for s in (0, 1):
            gcopy(part(at(0, 0), u), A1(u, s), n1(s)).start()

    def a1_wait(u):
        for s in (0, 1):
            gwait(part(at(3 if s == 0 else 1, 0), u), A1(u, s))

    def f1_send(u):
        for s in (0, 1):
            gcopy(part(at(3 if s == 0 else 1, 0), u, s), F1(u, s), n1(s)).start()

    def f1_wait(u):
        for s in (0, 1):
            gwait(part(at(2, 0), u, s), F1(u, s))

    def a2_send(u, m):
        for s in (0, 1):
            gcopy(part(at(SHIFT[m], 0), u), A2(u, m, s), n2(s)).start()

    def a2_wait(u, m):
        for s in (0, 1):
            gwait(part(at(SHIFT[m], 3 if s == 0 else 1), u), A2(u, m, s))

    def f2_send(u, m):
        for s in (0, 1):
            gcopy(part(at(SHIFT[m], 3 if s == 0 else 1), u, s), F2(u, m, s), n2(s)).start()

    def f2_wait(u, m):
        for s in (0, 1):
            gwait(part(at(SHIFT[m], 2), u, s), F2(u, m, s))

    def mate_send(pairs):
        for a, b in pairs:
            for s in (0, 1):
                gwait(beside(at(a, b), 1 - odd, s), ZED(a, b, s))
            gcopy(G.at[at(a, b), c], MATE(a, b), mate).start()

    def mate_wait(a, b):
        ref = G.at[at(a, b), 1 - c]
        pltpu.make_async_copy(ref, ref, grecv.at[MATE(b, a)]).wait()

    NEAR = ((1, 0), (3, 0), (0, 1), (0, 3))
    MID = ((2, 0), (0, 2), (3, 1), (3, 3))
    FAR = ((3, 2), (1, 1), (1, 3))
    LAST = ((2, 1), (2, 3), (1, 2))
    END = ((2, 2),)
    READY_MID = ((2, 0), (0, 2), (3, 3))
    READY_FAR = ((3, 1), (1, 1), (1, 3))
    READY_LAST = ((2, 3), (3, 2), (1, 2), (2, 1), (2, 2))

    def slot(n):
        if n in (0, 1):
            a1_send(n)
            a2_send(n, 0)
        elif n in (2, 3):
            u = n - 2
            a1_wait(u)
            f1_send(u)
            a2_wait(u, 0)
            f2_send(u, 0)
            a2_send(u, 1)
            if u == 1:
                z_send(NEAR)
        elif n == 4:
            a2_wait(0, 1)
            f2_send(0, 1)
            a2_send(0, 2)
            a2_send(1, 2)
            f1_wait(0)
            f2_wait(0, 0)
        elif n == 5:
            a2_wait(1, 1)
            f2_send(1, 1)
            f1_wait(1)
            a2_send(0, 3)
            a2_send(1, 3)
            f2_wait(1, 0)
            mate_send(NEAR)
            z_send(MID)
        elif n == 6:
            for u in (0, 1):
                a2_wait(u, 2)
                f2_send(u, 2)
                f2_wait(u, 1)
            z_send(FAR)
        elif n == 7:
            for u in (0, 1):
                a2_wait(u, 3)
                f2_send(u, 3)
            mate_send(MID)
        elif n == 8:
            f2_wait(0, 3)
            f2_wait(1, 3)
            z_send(END)
            mate_send(FAR)

    def late_slot():
        f2_wait(0, 2)
        f2_wait(1, 2)
        z_send(LAST)

    @pl.loop(0, 8)
    def _(k):
        rows = pl.ds(pl.multiple_of(k * 128, 128), 128)
        patch = lax.broadcasted_iota(jnp.int32, (128, R), 0) + k * 128
        oh[rows, :] = jnp.where(patch == mask[...], 1.0, 0.0).astype(BF16)

    def unit(patches):
        rows = lax.dot_general(oh[...], patches[...], (((0,), (0,)), ((), ())), preferred_element_type=F32)
        inverse = lax.rsqrt(jnp.sum(rows * rows, axis=1, keepdims=True) + EPS)
        return (rows * inverse).astype(BF16), inverse

    unit_s, inv_s = unit(student)
    su[...] = unit_s
    invn[...] = jnp.broadcast_to(inv_s, (R, 128))
    unit_t, _ = unit(teacher)
    tu[...] = unit_t
    for half in (0, 1):
        rows = slice(half * (R // 2), (half + 1) * (R // 2))
        G[i, half, 0] = su[rows, :].astype(F32)
        G[i, half, 1] = tu[rows, :].astype(F32)

    def x_send(it, k):
        for d in (2, 1, 3):
            send(csum.at[it, k], xr.at[it, k, d - 1], X0 + it * CH + k, along_x(d))

    for k in range(CH):
        proto_copy(k).wait()

        for n in range(CW // W):
            cols = slice(k * CW + n * W, k * CW + (n + 1) * W)
            w = nrm[:, cols].astype(F32)
            inverse = lax.rsqrt(jnp.sum(w * w, axis=0, keepdims=True) + EPS)
            unit_cols = (w * inverse).astype(BF16)
            colinv[:, cols] = inverse
            nrm[:, cols] = unit_cols
            e = jnp.exp2(nn(tu[...], unit_cols) * TEACHER)
            E[:, cols] = e
            csum[0, k, :, n * W:(n + 1) * W] = jnp.sum(e, axis=0, keepdims=True)

        if k == 2:
            pl.semaphore_wait(barrier, DP + HEAD - 2)
            for n in range(3):
                x_send(0, n)
    x_send(0, 3)

    mine = pl.ds(pl.multiple_of(i * W, W), W)
    nown[...] = nrm[:, mine]
    PU[...] = jnp.zeros_like(PU)
    U[...] = jnp.zeros_like(U)
    PG[...] = jnp.zeros_like(PG)
    eacc[...] = jnp.zeros_like(eacc)

    def tiles(v):
        total = v[:, 0:128]
        for t in range(1, v.shape[1] // 128):
            total = total + v[:, t * 128:(t + 1) * 128]
        return total

    def student_chunks(first, last):
        @pl.loop(first // 4, last // 4)
        def _(k):
            for n in range(4):
                cols = pl.ds(pl.multiple_of(k * 4 * W + n * W, W), W)
                unit_cols = nrm[:, cols]
                e = jnp.exp2(nn(su[...], unit_cols) * STUDENT)
                eacc[...] += tiles(e)
                PU[...] += nt(e.astype(BF16), unit_cols).reshape(DEEP, 2, S, B)

    def across(v):
        return jnp.sum(v.T, axis=0, keepdims=True)

    def down(v):
        return jnp.broadcast_to(v, (128, R)).T

    def y_step(it, k):
        landed(xr.at[it, k], X0 + it * CH + k)
        ysum[it, k] = csum[it, k] + xr[it, k, 0] + xr[it, k, 1] + xr[it, k, 2]
        for d in (2, 1, 3):
            send(ysum.at[it, k], yr.at[it, k, d - 1], Y0 + it * CH + k, along_y(d))

    def row_step(it, k):
        landed(yr.at[it, k], Y0 + it * CH + k)
        cs[:, k * CW:(k + 1) * CW] = 1.0 / (K * (ysum[it, k] + yr[it, k, 0] + yr[it, k, 1] + yr[it, k, 2]))
        if it < ITERS - 1:
            @pl.loop(0, R // 64)
            def _(n):
                rows = pl.ds(pl.multiple_of(n * 64, 64), 64)
                total = jnp.zeros((64, 128), F32) if k == 0 else racc[rows, :]
                for t in range(k * CW // 128, (k + 1) * CW // 128):
                    total = total + E[rows, t * 128:(t + 1) * 128] * cs[:, t * 128:(t + 1) * 128]
                racc[rows, :] = total

    def last_pass():
        racc[...] = jnp.zeros_like(racc)

        @pl.loop(0, 2)
        def _(k):
            for n in range(4):
                cols = pl.ds(pl.multiple_of(k * (C // 2) + n * LAST_W, LAST_W), LAST_W)
                t = E[:, cols] * cs[:, cols]
                racc[...] += tiles(t)
                U[...] += nt(t.astype(BF16), nrm[:, cols]).reshape(DEEP, 2, S, B)

    def col_step(it, k):
        @pl.loop(0, CW // 1024)
        def _(n):
            part = pl.ds(pl.multiple_of(n * 1024, 1024), 1024)
            cols = pl.ds(pl.multiple_of(k * CW + n * 1024, 1024), 1024)
            total = jnp.zeros((8, 1024), F32)
            for r in range(R // 8):
                scale = sscol[r * 8:(r + 1) * 8, :]
                total = total + E[r * 8:(r + 1) * 8, cols] * jnp.concatenate([scale] * 8, axis=1)
            csum[it, k, :, part] = jnp.sum(total, axis=0, keepdims=True)

    def block(a, b):
        blk = at(a, b)
        s = G[blk, :, 0].reshape(R, B).astype(BF16)
        t = G[blk, :, 1].reshape(R, B).astype(BF16)
        rows = pl.ds(pl.multiple_of(blk * R, R), R)
        ET[rows, :] = jnp.exp2(nn(t, nown[...]) * TEACHER).astype(BF16)
        e = jnp.exp2(nn(s, nown[...]) * STUDENT).astype(BF16)
        turned = s.astype(F32).T
        suT[:, rows] = turned.astype(BF16)
        PG[...] += nn((turned * iva[blk]).astype(BF16), e)

    def blocks(pairs):
        for a, b in pairs:
            if (a, b) != (0, 0):
                mate_wait(a, b)
            block(a, b)

    def core_sum_send(v, which, ph):
        send(v.at[:, 1 - c], cr.at[which], ph, mate)

    def core_sum_wait(v, which, ph, zph):
        landed(cr.at[which], ph)
        zs[which] = v[:, c] + cr[which]
        for d in range(1, DEEP):
            send(zs.at[which, lax.rem(z + d, DEEP)], zr.at[which, d - 1], zph, along_z(d))

    def z_sum(which, zph):
        landed(zr.at[which], zph)
        total = zs[which, z]
        for d in range(DEEP - 1):
            total = total + zr[which, d]
        return total

    for it in range(ITERS):
        slot(3 * it)
        if it == 0:
            student_chunks(0, 8)
        elif it == 1:
            core_sum_wait(PU, 0, CP, ZP)
        for k in range(CH):
            y_step(it, k)
        slot(3 * it + 1)
        if it == 0:
            student_chunks(8, 16)
        elif it == 1:
            landed(iva.at[pl.ds(0, DP - 1)], INV)
            blocks(((0, 0),))
        elif it == 2:
            blocks(READY_MID)
            late_slot()
        for k in range(CH):
            row_step(it, k)
        if it == ITERS - 1:
            last_pass()
            core_sum_send(U, 1, CU)
        hsrc[it, :, 0:R] = across(racc[...])
        if it == 0:
            hsrc[it, :, R:2 * R] = across(eacc[...])
        wide = 2 * R if it == 0 else R
        to_head(hsrc.at[it, :, pl.ds(0, wide)], lambda e: hr.at[it, e, :, pl.ds(0, wide)], H0 + it)
        slot(3 * it + 2)
        if it == 0:
            core_sum_send(PU, 0, CP)
        elif it == 1:
            blocks(NEAR)
        elif it == 2:
            core_sum_wait(U, 1, CU, ZU)
            blocks(READY_FAR)
        landed(hr.at[it, :, :, pl.ds(0, wide)], H0 + it)
        row_total = hsrc[it, :, 0:R]
        for d in range(HEAD - 1):
            row_total = row_total + hr[it, d, :, 0:R]
        if it == 0:
            exp_total = hsrc[it, :, R:2 * R]
            for d in range(HEAD - 1):
                exp_total = exp_total + hr[it, d, :, R:2 * R]
            iva[i] = 1.0 / exp_total
        if it < ITERS - 1:
            sscol[...] = down(1.0 / (ROWS * row_total))
            for k in range(CH):
                col_step(it + 1, k)
                x_send(it + 1, k)
        if it == 0:
            to_dp(iva.at[i], iva.at[i], INV)

    ssa[i] = 1.0 / row_total
    to_dp(ssa.at[i], ssa.at[i], SS)
    mate_send(LAST + END)
    blocks(READY_LAST)

    target_sum = z_sum(1, ZU)
    student_sum = z_sum(0, ZP)
    own = lax.broadcasted_iota(jnp.int32, (S, R), 1) == lax.broadcasted_iota(jnp.int32, (S, R), 0) + j * S

    def pick(v):
        return jnp.sum(jnp.where(own, v, 0.0), axis=1, keepdims=True)

    own_rows = pl.ds(pl.multiple_of(j * S, S), S)
    in_half = pl.ds(pl.multiple_of(lax.rem(j, 8) * S, S), S)
    unit_rows = G[i, j // 8, 0, in_half]
    target_mean = target_sum * pick(ssa[i])
    exp_inv = pick(iva[i])
    unit_grad = GRAD * (student_sum * exp_inv - target_mean)
    row_dot = jnp.sum(unit_rows * unit_grad, axis=1, keepdims=True)
    agb[c, z] = invn[own_rows, 0:1] * (unit_grad - unit_rows * row_dot)
    for d in (4, 3, 5, 2, 6, 1, 7):
        send(agb.at[c, z], agb.at[c, z], AGZ, along_z(d))
    raw_mean = jnp.sum(unit_rows * target_mean, axis=1, keepdims=True)
    part_loss = jnp.sum(raw_mean * 10.0 + jnp.log(exp_inv), axis=0, keepdims=True)
    ldr[i] = jnp.broadcast_to(part_loss, (1, 128))
    to_dp(ldr.at[i], ldr.at[i], LD)

    landed(ssa.at[pl.ds(0, DP - 1)], SS)
    for k in range(4):
        rows = slice(k * 4 * R, (k + 1) * 4 * R)
        scale = jnp.concatenate([ssa[k * 4 + n] for n in range(4)], axis=1)
        suT[:, rows] = (suT[:, rows].astype(F32) * scale).astype(BF16)

    @pl.loop(0, 2)
    def _(h):
        half = pl.ds(pl.multiple_of(h * (W // 2), W // 2), W // 2)
        mine_half = pl.ds(pl.multiple_of(i * W + h * (W // 2), W // 2), W // 2)
        grad = jnp.zeros((B, W // 2), F32)
        for k in range(4):
            rows = slice(k * 4 * R, (k + 1) * 4 * R)
            grad = grad + nn(suT[:, rows], ET[rows, half])
        unit_cols = nown[:, half].astype(F32)
        normed_grad = GRAD * (PG[:, half] - cs[:, mine_half] * grad)
        col_dot = jnp.sum(unit_cols * normed_grad, axis=0, keepdims=True)
        a2s[h] = (colinv[:, mine_half] * (normed_grad - unit_cols * col_dot)).reshape(DP, B // DP, W // 2)
        for a, b in DP_OFF:
            to = lax.rem(x + a, SIDE) * SIDE + lax.rem(y + b, SIDE)
            send(a2s.at[h, to], a2r.at[h, i], A2A + h, (to, j))
        a2r[h, i] = a2s[h, i]

    landed(ldr.at[pl.ds(0, DP - 1)], LD)
    total = ldr[0]
    for d in range(1, DP):
        total = total + ldr[d]
    lhr[j] = total
    to_head(lhr.at[j], lambda e: lhr.at[j], LH)
    landed(agb.at[c, pl.ds(0, DEEP - 1)], AGZ)
    send(agb.at[c], agb.at[c], AGC, mate)

    def rows_in(h):
        for k in range(DEEP):
            v = agb[h, k]
            high = v.astype(BF16)
            dhi[k, h] = high
            dlo[k, h] = (v - high.astype(F32)).astype(BF16)

    rows_in(c)
    landed(agb.at[1 - c], AGC)
    rows_in(1 - c)
    outs = []
    for n in range(4):
        rows = slice(n * 256, (n + 1) * 256)
        patch = nn(oh[rows, :], dhi[...].reshape(R, B)) + nn(oh[rows, :], dlo[...].reshape(R, B))
        E[0:256, n * 256:(n + 1) * 256] = patch
        outs.append(pltpu.make_async_copy(E.at[pl.ds(0, 256), pl.ds(n * 256, 256)], patch_out.at[pl.ds(n * 256, 256)], osem.at[n]))
        outs[-1].start()
    landed(lhr.at[pl.ds(0, HEAD - 1)], LH)
    total = lhr[0]
    for d in range(1, HEAD):
        total = total + lhr[d]
    loss_out[...] = total * (-1.0 / ROWS)

    for it in range(ITERS):
        for k in range(CH):
            sent(xr.at[it, k], X0 + it * CH + k)
            sent(yr.at[it, k], Y0 + it * CH + k)
        wide = 2 * R if it == 0 else R
        sent(hr.at[it, :, :, pl.ds(0, wide)], H0 + it)
    sent(iva.at[pl.ds(0, DP - 1)], INV)
    sent(ssa.at[pl.ds(0, DP - 1)], SS)
    sent(cr.at[1], CU)
    sent(cr.at[0], CP)
    sent(zr.at[1], ZU)
    sent(zr.at[0], ZP)
    sent(agb.at[c, pl.ds(0, DEEP - 1)], AGZ)
    sent(agb.at[c], AGC)
    sent(ldr.at[pl.ds(0, DP - 1)], LD)
    sent(lhr.at[pl.ds(0, HEAD - 1)], LH)
    whole, half, near = part(i, 0), part(i, 0, 0), beside(i, 0, 0)

    def gsent(like, sid):
        pltpu.make_async_copy(like, like, gsend.at[sid]).wait()

    for u in (0, 1):
        for s in (0, 1):
            gsent(whole, A1(u, s))
            gsent(half, F1(u, s))
            for m in range(4):
                gsent(whole, A2(u, m, s))
                gsent(half, F2(u, m, s))
    for a in range(SIDE):
        for b in range(SIDE):
            if (a, b) != (0, 0):
                gsent(G.at[i, c], MATE(a, b))
                gsent(near, ZED(a, b, 0))
                gsent(near, ZED(a, b, 1))

    for h in (0, 1):
        landed(a2r.at[h, pl.ds(0, DP - 1)], A2A + h)
        for d in range(DP):
            wide_out[:, d * W + h * W // 2:d * W + (h + 1) * W // 2] = a2r[h, d]
    outs.append(pltpu.make_async_copy(wide_out, proto_out, osem.at[4]))
    outs[-1].start()
    for h in (0, 1):
        sent(a2r.at[h, pl.ds(0, DP - 1)], A2A + h)
    for copy in outs:
        copy.wait()


def finish(patches, protos, patch_out, proto_out, patch_buf, proto_buf, isem, osem):
    parts = []
    for source, buf, target, count in ((patches, patch_buf, patch_out, 4), (protos, proto_buf, proto_out, 2)):
        size = source.shape[0] // count
        for n in range(count):
            rows, at = pl.ds(n * size, size), len(parts)
            parts.append((
                pltpu.make_async_copy(source.at[rows], buf.at[rows], isem.at[at]),
                pltpu.make_async_copy(buf.at[rows], target.at[rows], osem.at[at]),
            ))
    for get, _ in parts:
        get.start()
    for get, put in parts:
        get.wait()
        put.start()
    for _, put in parts:
        put.wait()


def on_device(student_patches, teacher_patches, mask_rows, prototypes):
    vm = pltpu.VMEM
    whole = pl.BlockSpec(memory_space=pltpu.VMEM)
    anywhere = pl.BlockSpec(memory_space=pl.ANY)
    results = (
        jax.ShapeDtypeStruct(student_patches.shape, F32),
        jax.ShapeDtypeStruct((B // DP, C), F32),
    )
    patches, protos, loss = pl.pallas_call(
        kernel,
        out_shape=results + (jax.ShapeDtypeStruct((1, 128), F32),),
        in_specs=[whole] * 3 + [anywhere],
        out_specs=(anywhere, anywhere, whole),
        scratch_shapes=[
            vm((1024, R), BF16),
            vm((R, B), BF16),
            vm((R, B), BF16),
            vm((R, 128), F32),
            vm((B, C), BF16),
            vm((B, W), BF16),
            vm((1, C), F32),
            vm((R, C), F32),
            vm((DP, 2, 2, R // 2, B), F32),
            vm((DP * R, W), BF16),
            vm((B, DP * R), BF16),
            vm((B, W), F32),
            vm((DEEP, 2, S, B), F32),
            vm((DEEP, 2, S, B), F32),
            vm((2, DEEP, S, B), F32),
            vm((2, DEEP, S, B), F32),
            vm((2, DEEP - 1, S, B), F32),
            vm((ITERS, CH, 1, CW), F32),
            vm((ITERS, CH, 1, CW), F32),
            vm((ITERS, CH, SIDE - 1, 1, CW), F32),
            vm((ITERS, CH, SIDE - 1, 1, CW), F32),
            vm((1, C), F32),
            vm((R, 128), F32),
            vm((R, 128), F32),
            vm((R, 128), F32),
            vm((ITERS, 1, 2 * R), F32),
            vm((ITERS, HEAD - 1, 1, 2 * R), F32),
            vm((DP, 1, R), F32),
            vm((DP, 1, R), F32),
            vm((2, DEEP, S, B), F32),
            vm((2, DP, B // DP, W // 2), F32),
            vm((2, DP, B // DP, W // 2), F32),
            vm((B // DP, C), F32),
            vm((DEEP, 2, S, B), BF16),
            vm((DEEP, 2, S, B), BF16),
            vm((DP, 1, 128), F32),
            vm((HEAD, 1, 128), F32),
            pltpu.SemaphoreType.DMA((SMALL,)),
            pltpu.SemaphoreType.DMA((SMALL,)),
            pltpu.SemaphoreType.DMA((GATHER,)),
            pltpu.SemaphoreType.DMA((GATHER,)),
            pltpu.SemaphoreType.DMA((CH,)),
            pltpu.SemaphoreType.DMA((5,)),
        ],
        compiler_params=pltpu.CompilerParams(
            collective_id=0, has_side_effects=True, vmem_limit_bytes=63 * 2**20
        ),
    )(student_patches, teacher_patches, mask_rows.reshape(1, R), prototypes)
    patches, protos = pl.pallas_call(
        finish,
        out_shape=results,
        in_specs=[anywhere] * 2,
        out_specs=(anywhere, anywhere),
        scratch_shapes=[
            vm(student_patches.shape, F32),
            vm((B // DP, C), F32),
            pltpu.SemaphoreType.DMA((6,)),
            pltpu.SemaphoreType.DMA((6,)),
        ],
    )(patches, protos)
    return patches, protos, loss[0, 0]


def solution(mesh):
    return jax.shard_map(
        on_device,
        mesh=mesh,
        in_specs=(P("dp", None), P("dp", None), P("dp"), P(None, "head")),
        out_specs=(P("dp", None), P("dp", "head"), P()),
        check_vma=False,
    )
```

```python
import functools
import math

import jax
import jax.numpy as jnp
from jax import lax
from jax.experimental import pallas as pl
from jax.experimental.pallas import tpu as pltpu
from jax.sharding import PartitionSpec as P

MESH = pl.DeviceIdType.MESH
F32, BF16 = jnp.float32, jnp.bfloat16

EPS = 1e-06
LOG2E = math.log2(math.e)
TEACHER = 25.0 * LOG2E
STUDENT = 10.0 * LOG2E
GRAD = 4096.0 / 0.1
ITERS = 3
DP, HEAD, SIDE, DEEP = 16, 16, 4, 8
R, B, C = 512, 256, 8192
W = C // DP
ROWS, K = R * DP, C * HEAD
S = R // HEAD

CH = 4
CW = C // CH
LAST_W = 1024
X0, Y0, H0 = 0, ITERS * CH, 2 * ITERS * CH
INV, SS, CU, ZU, CP, ZP, AGZ, AGC, LD, LH, A2A = range(H0 + ITERS, H0 + ITERS + 11)
SMALL = A2A + 2
XS, YS = X0, Y0


def far_first(sides):
    offsets = [(a, b) for a in range(sides[0]) for b in range(sides[1]) if (a, b) != (0, 0)]
    return sorted(offsets, key=lambda o: -min(o[0], sides[0] - o[0]) - min(o[1], sides[1] - o[1]))


DP_OFF, HEAD_OFF = far_first((SIDE, SIDE)), far_first((DEEP, 2))

A1, F1 = lambda u: u, lambda u: 2 + u
A2, F2 = lambda u, m: 4 + u * 4 + m, lambda u, m: 12 + u * 4 + m
MATE = lambda a, b: 20 + a * 4 + b
ZED = 36
GATHER = 41
WHOLE, HALF, MATES, BESIDES = range(4)
PLANE, BESIDE = 176, 80
SHIFT = (0, 3, 1, 2)


def nt(a, b):
    return lax.dot_general(a, b, (((1,), (1,)), ((), ())), preferred_element_type=F32)


def nn(a, b):
    return jnp.dot(a, b, preferred_element_type=F32)


def kernel(student_hbm, teacher_hbm, mask_hbm, proto, patch_out, proto_out, loss_out,
           student, teacher, mask, loss, oh, su, tu, invn, nrm, nown, colinv, E, G, ET, suT, PG,
           U, PU, cr, zs, zr, csum, ysum, xr, yr, cs, racc, eacc, sscol,
           hsrc, hr, iva, ssa, agb, a2s, a2r, wide_out, dhi, dlo, ldr, lhr,
           psend, precv, gsend, grecv, lsem, osem):
    i, j = lax.axis_index("dp"), lax.axis_index("head")
    x, y = i // SIDE, lax.rem(i, SIDE)
    z, c = j // 2, lax.rem(j, 2)
    mate = (i, z * 2 + 1 - c)

    def proto_copy(k):
        cols = pl.ds(k * CW, CW)
        return pltpu.make_async_copy(proto.at[:, cols], nrm.at[:, cols], lsem.at[k])

    def patch_copy(k):
        return pltpu.make_async_copy((teacher_hbm, student_hbm)[k], (teacher, student)[k], lsem.at[CH + k])

    mask_copy = pltpu.make_async_copy(mask_hbm, mask, lsem.at[CH + 2])

    barrier = pltpu.get_barrier_semaphore()
    mask_copy.start()
    for k in (0, 1):
        patch_copy(k).start()
    for k in range(CH):
        proto_copy(k).start()
    for d in range(1, DP):
        pl.semaphore_signal(barrier, inc=1, device_id=(lax.rem(i + d, DP), j), device_id_type=MESH)
        pl.semaphore_signal(barrier, inc=1, device_id=(i, lax.rem(j + d, HEAD)), device_id_type=MESH)

    def send(src, dst, ph, dev, leave=None):
        leave = ph if leave is None else leave
        pltpu.make_async_remote_copy(src, dst, psend.at[leave], precv.at[ph], device_id=dev, device_id_type=MESH).start()

    def landed(like, ph):
        pltpu.make_async_copy(like, like, precv.at[ph]).wait()

    def sent(like, ph):
        pltpu.make_async_copy(like, like, psend.at[ph]).wait()

    def along_x(d):
        return (lax.rem(x + d, SIDE) * SIDE + y, j)

    def along_y(d):
        return (x * SIDE + lax.rem(y + d, SIDE), j)

    def to_dp(src, dst, ph):
        for a, b in DP_OFF:
            send(src, dst, ph, (lax.rem(x + a, SIDE) * SIDE + lax.rem(y + b, SIDE), j))

    def to_head(src, dst, ph):
        for e, (a, b) in enumerate(HEAD_OFF):
            send(src, dst(e), ph, (i, lax.rem(z + a, DEEP) * 2 + lax.rem(c + b, 2)))

    def along_z(d):
        return (i, lax.rem(z + d, DEEP) * 2 + c)

    p = x * (1 - c) + y * c
    q = y * (1 - c) + x * c

    def at(dp_, dq_):
        pp, qq = lax.rem(p + dp_, SIDE), lax.rem(q + dq_, SIDE)
        return (pp * SIDE + qq) * (1 - c) + (qq * SIDE + pp) * c

    odd = lax.rem(z, 2)

    def part(blk, u, half=None):
        first = odd * BESIDE + (0 if half is None else half * (PLANE // 2))
        rows = pl.ds(pl.multiple_of(first, 8), PLANE if half is None else PLANE // 2)
        return G.at[blk, c, u, rows]

    def beside(blk, which, s):
        first = which * PLANE + s * (BESIDE // 2)
        return G.at[blk, c, :, pl.ds(pl.multiple_of(first, 8), BESIDE // 2)]

    def gcopy(ref, kind, sid, dev):
        pltpu.make_async_remote_copy(ref, ref, gsend.at[kind], grecv.at[sid], device_id=dev, device_id_type=MESH).start()

    def gwait(like, sid):
        pltpu.make_async_copy(like, like, grecv.at[sid]).wait()

    both = G.at[0, c, :, pl.ds(0, PLANE)]
    both_halves = G.at[0, c, :, pl.ds(0, PLANE // 2)]

    def z_send(pairs, batch):
        for a, b in pairs:
            for s in (0, 1):
                gcopy(beside(at(a, b), odd, s), BESIDES, ZED + batch, along_z(1 if s == 0 else DEEP - 1))

    def n1(s):
        return (at(1 if s == 0 else 3, 0), j)

    def n2(s):
        return (at(0, 1 if s == 0 else 3), j)

    def a1_send(u):
        for s in (0, 1):
            gcopy(part(at(0, 0), u), WHOLE, A1(u), n1(s))

    def a1_wait(u):
        gwait(both, A1(u))

    def f1_send(u):
        for s in (0, 1):
            gcopy(part(at(3 if s == 0 else 1, 0), u, s), HALF, F1(u), n1(s))

    def f1_wait(u):
        gwait(both_halves, F1(u))

    def a2_send(u, m):
        for s in (0, 1):
            gcopy(part(at(SHIFT[m], 0), u), WHOLE, A2(u, m), n2(s))

    def a2_wait(u, m):
        gwait(both, A2(u, m))

    def f2_send(u, m):
        for s in (0, 1):
            gcopy(part(at(SHIFT[m], 3 if s == 0 else 1), u, s), HALF, F2(u, m), n2(s))

    def f2_wait(u, m):
        gwait(both_halves, F2(u, m))

    def mate_send(pairs, batch):
        gwait(G.at[pl.ds(0, len(pairs)), c, :, pl.ds(0, BESIDE)], ZED + batch)
        for a, b in pairs:
            gcopy(G.at[at(a, b), c], MATES, MATE(a, b), mate)

    def mate_wait(a, b):
        gwait(G.at[0, c], MATE(b, a))

    NEAR = ((1, 0), (3, 0), (0, 1), (0, 3))
    MID = ((2, 0), (0, 2), (3, 1), (3, 3))
    FAR = ((3, 2), (1, 1), (1, 3))
    LAST = ((2, 1), (2, 3), (1, 2))
    END = ((2, 2),)
    READY_MID = ((2, 0), (0, 2), (3, 3))
    READY_FAR = ((3, 1), (1, 1), (1, 3))
    READY_LAST = ((2, 3), (3, 2), (1, 2), (2, 1))

    def slot(n):
        if n in (0, 1):
            a1_send(n)
            a2_send(n, 0)
        elif n == 2:
            a1_wait(0)
            f1_send(0)
            a2_wait(0, 0)
            f2_send(0, 0)
            a2_send(0, 1)
        elif n == 3:
            a2_send(1, 1)
        elif n == 4:
            a2_wait(0, 1)
            f2_send(0, 1)
            a2_send(0, 2)
            a2_send(1, 2)
            f1_wait(0)
            f2_wait(0, 0)
        elif n == 5:
            a2_wait(1, 1)
            f2_send(1, 1)
            f1_wait(1)
            a2_send(0, 3)
            a2_send(1, 3)
            f2_wait(1, 0)
            z_send(MID, 1)
        elif n == 6:
            for u in (0, 1):
                a2_wait(u, 3)
                f2_send(u, 3)
                f2_wait(u, 2)
            z_send(LAST, 3)
        elif n == 7:
            mate_send(MID, 1)
        elif n == 8:
            mate_send(FAR, 2)
            f2_wait(0, 3)
            f2_wait(1, 3)
            z_send(END, 4)

    def later_slot(n):
        if n == 2:
            a1_wait(1)
            f1_send(1)
            a2_wait(1, 0)
            f2_send(1, 0)
            z_send(NEAR, 0)
        elif n == 4:
            mate_send(NEAR, 0)
        elif n == 5:
            for u in (0, 1):
                a2_wait(u, 2)
                f2_send(u, 2)
                f2_wait(u, 1)
            z_send(FAR, 2)
        elif n == 8:
            mate_send(LAST, 3)

    mask_copy.wait()

    @pl.loop(0, 8)
    def _(k):
        rows = pl.ds(pl.multiple_of(k * 128, 128), 128)
        patch = lax.broadcasted_iota(jnp.int32, (128, R), 0) + k * 128
        oh[rows, :] = jnp.where(patch == mask[...], 1.0, 0.0).astype(BF16)

    def unit(patches):
        rows = lax.dot_general(oh[...], patches[...], (((0,), (0,)), ((), ())), preferred_element_type=F32)
        inverse = lax.rsqrt(jnp.sum(rows * rows, axis=1, keepdims=True) + EPS)
        return (rows * inverse).astype(BF16), inverse

    patch_copy(0).wait()
    unit_t, _ = unit(teacher)
    tu[...] = unit_t
    patch_copy(1).wait()
    unit_s, inv_s = unit(student)
    su[...] = unit_s
    invn[...] = jnp.broadcast_to(inv_s, (R, 128))
    for half in (0, 1):
        rows = slice(half * (R // 2), (half + 1) * (R // 2))
        G[i, half, 0] = su[rows, :].astype(F32)
        G[i, half, 1] = tu[rows, :].astype(F32)

    def x_send(it, k):
        for d in (2, 1, 3):
            send(csum.at[it, k], xr.at[it, k, d - 1], X0 + it * CH + k, along_x(d), XS)

    for k in range(CH):
        proto_copy(k).wait()

        for n in range(CW // W):
            cols = slice(k * CW + n * W, k * CW + (n + 1) * W)
            w = nrm[:, cols].astype(F32)
            inverse = lax.rsqrt(jnp.sum(w * w, axis=0, keepdims=True) + EPS)
            unit_cols = (w * inverse).astype(BF16)
            colinv[:, cols] = inverse
            nrm[:, cols] = unit_cols
            e = jnp.exp2(nn(tu[...], unit_cols) * TEACHER)
            E[:, cols] = e
            csum[0, k, :, n * W:(n + 1) * W] = jnp.sum(e, axis=0, keepdims=True)

        if k == 2:
            pl.semaphore_wait(barrier, DP + HEAD - 2)
            for n in range(3):
                x_send(0, n)
    x_send(0, 3)

    mine = pl.ds(pl.multiple_of(i * W, W), W)
    nown[...] = nrm[:, mine]
    PU[...] = jnp.zeros_like(PU)
    U[...] = jnp.zeros_like(U)
    PG[...] = jnp.zeros_like(PG)
    eacc[...] = jnp.zeros_like(eacc)

    def tiles(v):
        total = v[:, 0:128]
        for t in range(1, v.shape[1] // 128):
            total = total + v[:, t * 128:(t + 1) * 128]
        return total

    def student_chunks(first, last):
        @pl.loop(first // 4, last // 4)
        def _(k):
            for n in range(4):
                cols = pl.ds(pl.multiple_of(k * 4 * W + n * W, W), W)
                unit_cols = nrm[:, cols]
                e = jnp.exp2(nn(su[...], unit_cols) * STUDENT)
                eacc[...] += tiles(e)
                PU[...] += nt(e.astype(BF16), unit_cols).reshape(DEEP, 2, S, B)

    def across(v):
        return jnp.sum(v.T, axis=0, keepdims=True)

    def down(v):
        return jnp.broadcast_to(v, (128, R)).T

    def y_step(it, k):
        landed(xr.at[it, k], X0 + it * CH + k)
        ysum[it, k] = csum[it, k] + xr[it, k, 0] + xr[it, k, 1] + xr[it, k, 2]
        for d in (2, 1, 3):
            send(ysum.at[it, k], yr.at[it, k, d - 1], Y0 + it * CH + k, along_y(d), YS)

    def row_step(it, k):
        landed(yr.at[it, k], Y0 + it * CH + k)
        cs[:, k * CW:(k + 1) * CW] = 1.0 / (K * (ysum[it, k] + yr[it, k, 0] + yr[it, k, 1] + yr[it, k, 2]))
        if it < ITERS - 1:
            @pl.loop(0, R // 64)
            def _(n):
                rows = pl.ds(pl.multiple_of(n * 64, 64), 64)
                total = jnp.zeros((64, 128), F32) if k == 0 else racc[rows, :]
                for t in range(k * CW // 128, (k + 1) * CW // 128):
                    total = total + E[rows, t * 128:(t + 1) * 128] * cs[:, t * 128:(t + 1) * 128]
                racc[rows, :] = total

    def last_pass():
        racc[...] = jnp.zeros_like(racc)

        @pl.loop(0, 2)
        def _(k):
            for n in range(4):
                cols = pl.ds(pl.multiple_of(k * (C // 2) + n * LAST_W, LAST_W), LAST_W)
                t = E[:, cols] * cs[:, cols]
                racc[...] += tiles(t)
                U[...] += nt(t.astype(BF16), nrm[:, cols]).reshape(DEEP, 2, S, B)

    def col_step(it, k):
        @pl.loop(0, CW // 1024)
        def _(n):
            part = pl.ds(pl.multiple_of(n * 1024, 1024), 1024)
            cols = pl.ds(pl.multiple_of(k * CW + n * 1024, 1024), 1024)
            total = jnp.zeros((8, 1024), F32)
            for r in range(R // 8):
                scale = sscol[r * 8:(r + 1) * 8, :]
                total = total + E[r * 8:(r + 1) * 8, cols] * jnp.concatenate([scale] * 8, axis=1)
            csum[it, k, :, part] = jnp.sum(total, axis=0, keepdims=True)

    def block(a, b):
        blk = at(a, b)
        s = G[blk, :, 0].reshape(R, B).astype(BF16)
        t = G[blk, :, 1].reshape(R, B).astype(BF16)
        rows = pl.ds(pl.multiple_of(blk * R, R), R)
        ET[rows, :] = jnp.exp2(nn(t, nown[...]) * TEACHER).astype(BF16)
        e = jnp.exp2(nn(s, nown[...]) * STUDENT).astype(BF16)
        turned = s.astype(F32).T
        suT[:, rows] = turned.astype(BF16)
        PG[...] += nn((turned * iva[blk]).astype(BF16), e)

    def blocks(pairs):
        for a, b in pairs:
            if (a, b) != (0, 0):
                mate_wait(a, b)
            block(a, b)

    def core_sum_send(v, which, ph):
        send(v.at[:, 1 - c], cr.at[which], ph, mate)

    def core_sum_wait(v, which, ph, zph):
        landed(cr.at[which], ph)
        zs[which] = v[:, c] + cr[which]
        for d in range(1, DEEP):
            send(zs.at[which, lax.rem(z + d, DEEP)], zr.at[which, d - 1], zph, along_z(d))

    def z_sum(which, zph):
        landed(zr.at[which], zph)
        total = zs[which, z]
        for d in range(DEEP - 1):
            total = total + zr[which, d]
        return total

    for it in range(ITERS):
        slot(3 * it)
        if it == 0:
            student_chunks(0, 8)
        elif it == 1:
            core_sum_wait(PU, 0, CP, ZP)
        for k in range(CH):
            y_step(it, k)
        slot(3 * it + 1)
        if it == 0:
            student_chunks(8, 16)
        elif it == 1:
            landed(iva.at[pl.ds(0, DP - 1)], INV)
            blocks(((0, 0),))
            later_slot(4)
        elif it == 2:
            blocks(READY_MID)
        for k in range(CH):
            row_step(it, k)
        if it == ITERS - 1:
            last_pass()
            core_sum_send(U, 1, CU)
        hsrc[it, :, 0:R] = across(racc[...])
        if it == 0:
            hsrc[it, :, R:2 * R] = across(eacc[...])
        wide = 2 * R if it == 0 else R
        to_head(hsrc.at[it, :, pl.ds(0, wide)], lambda e: hr.at[it, e, :, pl.ds(0, wide)], H0 + it)
        slot(3 * it + 2)
        if it == 0:
            core_sum_send(PU, 0, CP)
            later_slot(2)
        elif it == 1:
            blocks(NEAR)
            later_slot(5)
        elif it == 2:
            core_sum_wait(U, 1, CU, ZU)
            blocks(READY_FAR)
            later_slot(8)
        landed(hr.at[it, :, :, pl.ds(0, wide)], H0 + it)
        row_total = hsrc[it, :, 0:R]
        for d in range(HEAD - 1):
            row_total = row_total + hr[it, d, :, 0:R]
        if it == 0:
            exp_total = hsrc[it, :, R:2 * R]
            for d in range(HEAD - 1):
                exp_total = exp_total + hr[it, d, :, R:2 * R]
            iva[i] = 1.0 / exp_total
        if it < ITERS - 1:
            sscol[...] = down(1.0 / (ROWS * row_total))
            for k in range(CH):
                col_step(it + 1, k)
                x_send(it + 1, k)
        if it == 0:
            to_dp(iva.at[i], iva.at[i], INV)

    ssa[i] = 1.0 / row_total
    to_dp(ssa.at[i], ssa.at[i], SS)
    blocks(READY_LAST[:2])
    mate_send(END, 4)
    blocks(READY_LAST[2:] + END)

    target_sum = z_sum(1, ZU)
    student_sum = z_sum(0, ZP)
    own = lax.broadcasted_iota(jnp.int32, (S, R), 1) == lax.broadcasted_iota(jnp.int32, (S, R), 0) + j * S

    def pick(v):
        return jnp.sum(jnp.where(own, v, 0.0), axis=1, keepdims=True)

    own_rows = pl.ds(pl.multiple_of(j * S, S), S)
    in_half = pl.ds(pl.multiple_of(lax.rem(j, 8) * S, S), S)
    unit_rows = G[i, j // 8, 0, in_half]
    target_mean = target_sum * pick(ssa[i])
    exp_inv = pick(iva[i])
    unit_grad = GRAD * (student_sum * exp_inv - target_mean)
    row_dot = jnp.sum(unit_rows * unit_grad, axis=1, keepdims=True)
    agb[c, z] = invn[own_rows, 0:1] * (unit_grad - unit_rows * row_dot)
    for d in (4, 3, 5, 2, 6, 1, 7):
        send(agb.at[c, z], agb.at[c, z], AGZ, along_z(d))
    raw_mean = jnp.sum(unit_rows * target_mean, axis=1, keepdims=True)
    part_loss = jnp.sum(raw_mean * 10.0 + jnp.log(exp_inv), axis=0, keepdims=True)
    ldr[i] = jnp.broadcast_to(part_loss, (1, 128))
    to_dp(ldr.at[i], ldr.at[i], LD)

    landed(ssa.at[pl.ds(0, DP - 1)], SS)
    for k in range(4):
        rows = slice(k * 4 * R, (k + 1) * 4 * R)
        scale = jnp.concatenate([ssa[k * 4 + n] for n in range(4)], axis=1)
        suT[:, rows] = (suT[:, rows].astype(F32) * scale).astype(BF16)

    @pl.loop(0, 2)
    def _(h):
        half = pl.ds(pl.multiple_of(h * (W // 2), W // 2), W // 2)
        mine_half = pl.ds(pl.multiple_of(i * W + h * (W // 2), W // 2), W // 2)
        grad = jnp.zeros((B, W // 2), F32)
        for k in range(4):
            rows = slice(k * 4 * R, (k + 1) * 4 * R)
            grad = grad + nn(suT[:, rows], ET[rows, half])
        unit_cols = nown[:, half].astype(F32)
        normed_grad = GRAD * (PG[:, half] - cs[:, mine_half] * grad)
        col_dot = jnp.sum(unit_cols * normed_grad, axis=0, keepdims=True)
        a2s[h] = (colinv[:, mine_half] * (normed_grad - unit_cols * col_dot)).reshape(DP, B // DP, W // 2)
        for a, b in DP_OFF:
            to = lax.rem(x + a, SIDE) * SIDE + lax.rem(y + b, SIDE)
            send(a2s.at[h, to], a2r.at[h, i], A2A + h, (to, j))
        a2r[h, i] = a2s[h, i]

    landed(ldr.at[pl.ds(0, DP - 1)], LD)
    total = ldr[0]
    for d in range(1, DP):
        total = total + ldr[d]
    lhr[j] = total
    to_head(lhr.at[j], lambda e: lhr.at[j], LH)
    landed(agb.at[c, pl.ds(0, DEEP - 1)], AGZ)
    send(agb.at[c], agb.at[c], AGC, mate)

    def rows_in(h):
        for k in range(DEEP):
            v = agb[h, k]
            high = v.astype(BF16)
            dhi[k, h] = high
            dlo[k, h] = (v - high.astype(F32)).astype(BF16)

    rows_in(c)
    landed(agb.at[1 - c], AGC)
    rows_in(1 - c)
    outs = []
    for n in range(4):
        rows = slice(n * 256, (n + 1) * 256)
        patch = nn(oh[rows, :], dhi[...].reshape(R, B)) + nn(oh[rows, :], dlo[...].reshape(R, B))
        E[0:256, n * 256:(n + 1) * 256] = patch
        outs.append(pltpu.make_async_copy(E.at[pl.ds(0, 256), pl.ds(n * 256, 256)], patch_out.at[pl.ds(n * 256, 256)], osem.at[n]))
        outs[-1].start()
    landed(lhr.at[pl.ds(0, HEAD - 1)], LH)
    total = lhr[0]
    for d in range(1, HEAD):
        total = total + lhr[d]
    loss[...] = total * (-1.0 / ROWS)
    outs.append(pltpu.make_async_copy(loss, loss_out, osem.at[5]))
    outs[-1].start()

    sent(xr, XS)
    sent(yr, YS)
    for it in range(ITERS):
        wide = 2 * R if it == 0 else R
        sent(hr.at[it, :, :, pl.ds(0, wide)], H0 + it)
    sent(iva.at[pl.ds(0, DP - 1)], INV)
    sent(ssa.at[pl.ds(0, DP - 1)], SS)
    sent(cr.at[1], CU)
    sent(cr.at[0], CP)
    sent(zr.at[1], ZU)
    sent(zr.at[0], ZP)
    sent(agb.at[c, pl.ds(0, DEEP - 1)], AGZ)
    sent(agb.at[c], AGC)
    sent(ldr.at[pl.ds(0, DP - 1)], LD)
    sent(lhr.at[pl.ds(0, HEAD - 1)], LH)

    def gsent(like, kind):
        pltpu.make_async_copy(like, like, gsend.at[kind]).wait()

    gsent(G.at[pl.ds(0, 10), c, :, pl.ds(0, PLANE)], WHOLE)
    gsent(G.at[pl.ds(0, 10), c, :, pl.ds(0, PLANE // 2)], HALF)
    gsent(G.at[pl.ds(0, DP - 1), c], MATES)
    gsent(G.at[pl.ds(0, DP - 1), c, :, pl.ds(0, BESIDE)], BESIDES)

    for h in (0, 1):
        landed(a2r.at[h, pl.ds(0, DP - 1)], A2A + h)
        for d in range(DP):
            wide_out[:, d * W + h * W // 2:d * W + (h + 1) * W // 2] = a2r[h, d]
    outs.append(pltpu.make_async_copy(wide_out, proto_out, osem.at[4]))
    outs[-1].start()
    for h in (0, 1):
        sent(a2r.at[h, pl.ds(0, DP - 1)], A2A + h)
    for copy in outs:
        copy.wait()


def finish(patches, protos, patch_out, proto_out, patch_buf, proto_buf, isem, osem):
    parts = []
    for source, buf, target, count in ((patches, patch_buf, patch_out, 4), (protos, proto_buf, proto_out, 2)):
        size = source.shape[0] // count
        for n in range(count):
            rows, at = pl.ds(n * size, size), len(parts)
            parts.append((
                pltpu.make_async_copy(source.at[rows], buf.at[rows], isem.at[at]),
                pltpu.make_async_copy(buf.at[rows], target.at[rows], osem.at[at]),
            ))
    for get, _ in parts:
        get.start()
    for get, put in parts:
        get.wait()
        put.start()
    for _, put in parts:
        put.wait()


def on_device(student_patches, teacher_patches, mask_rows, prototypes):
    vm = pltpu.VMEM
    anywhere = pl.BlockSpec(memory_space=pl.ANY)
    results = (
        jax.ShapeDtypeStruct(student_patches.shape, F32),
        jax.ShapeDtypeStruct((B // DP, C), F32),
    )
    patches, protos, loss = pl.pallas_call(
        kernel,
        out_shape=results + (jax.ShapeDtypeStruct((1, 128), F32),),
        in_specs=[anywhere] * 4,
        out_specs=(anywhere,) * 3,
        scratch_shapes=[
            vm(student_patches.shape, BF16),
            vm(student_patches.shape, BF16),
            vm((1, R), jnp.int32),
            vm((1, 128), F32),
            vm((1024, R), BF16),
            vm((R, B), BF16),
            vm((R, B), BF16),
            vm((R, 128), F32),
            vm((B, C), BF16),
            vm((B, W), BF16),
            vm((1, C), F32),
            vm((R, C), F32),
            vm((DP, 2, 2, R // 2, B), F32),
            vm((DP * R, W), BF16),
            vm((B, DP * R), BF16),
            vm((B, W), F32),
            vm((DEEP, 2, S, B), F32),
            vm((DEEP, 2, S, B), F32),
            vm((2, DEEP, S, B), F32),
            vm((2, DEEP, S, B), F32),
            vm((2, DEEP - 1, S, B), F32),
            vm((ITERS, CH, 1, CW), F32),
            vm((ITERS, CH, 1, CW), F32),
            vm((ITERS, CH, SIDE - 1, 1, CW), F32),
            vm((ITERS, CH, SIDE - 1, 1, CW), F32),
            vm((1, C), F32),
            vm((R, 128), F32),
            vm((R, 128), F32),
            vm((R, 128), F32),
            vm((ITERS, 1, 2 * R), F32),
            vm((ITERS, HEAD - 1, 1, 2 * R), F32),
            vm((DP, 1, R), F32),
            vm((DP, 1, R), F32),
            vm((2, DEEP, S, B), F32),
            vm((2, DP, B // DP, W // 2), F32),
            vm((2, DP, B // DP, W // 2), F32),
            vm((B // DP, C), F32),
            vm((DEEP, 2, S, B), BF16),
            vm((DEEP, 2, S, B), BF16),
            vm((DP, 1, 128), F32),
            vm((HEAD, 1, 128), F32),
            pltpu.SemaphoreType.DMA((SMALL,)),
            pltpu.SemaphoreType.DMA((SMALL,)),
            pltpu.SemaphoreType.DMA((4,)),
            pltpu.SemaphoreType.DMA((GATHER,)),
            pltpu.SemaphoreType.DMA((CH + 3,)),
            pltpu.SemaphoreType.DMA((6,)),
        ],
        compiler_params=pltpu.CompilerParams(
            collective_id=0, has_side_effects=True, vmem_limit_bytes=63 * 2**20
        ),
    )(student_patches, teacher_patches, mask_rows.reshape(1, R), prototypes)
    patches, protos = pl.pallas_call(
        finish,
        out_shape=results,
        in_specs=[anywhere] * 2,
        out_specs=(anywhere, anywhere),
        scratch_shapes=[
            vm(student_patches.shape, F32),
            vm((B // DP, C), F32),
            pltpu.SemaphoreType.DMA((6,)),
            pltpu.SemaphoreType.DMA((6,)),
        ],
    )(patches, protos)
    return patches, protos, loss[0, 0]


def solution(mesh):
    return jax.shard_map(
        on_device,
        mesh=mesh,
        in_specs=(P("dp", None), P("dp", None), P("dp"), P(None, "head")),
        out_specs=(P("dp", None), P("dp", "head"), P()),
        check_vma=False,
    )
```

```python
import functools
import math

import jax
import jax.numpy as jnp
from jax import lax
from jax.experimental import pallas as pl
from jax.experimental.pallas import tpu as pltpu
from jax.sharding import PartitionSpec as P

MESH = pl.DeviceIdType.MESH
F32, BF16 = jnp.float32, jnp.bfloat16

EPS = 1e-06
LOG2E = math.log2(math.e)
TEACHER = 25.0 * LOG2E
STUDENT = 10.0 * LOG2E
GRAD = 4096.0 / 0.1
ITERS = 3
DP, HEAD, SIDE, DEEP = 16, 16, 4, 8
R, B, C = 512, 256, 8192
W = C // DP
ROWS, K = R * DP, C * HEAD
S = R // HEAD

CH = 4
CW = C // CH
LAST_W = 1024
X0, Y0, H0 = 0, ITERS * CH, 2 * ITERS * CH
INV, SS, CU, ZU, CP, ZP, AGZ, AGC, LD, LH, A2A = range(H0 + ITERS, H0 + ITERS + 11)
SMALL = A2A + 2
XS, YS = X0, Y0


def far_first(sides):
    offsets = [(a, b) for a in range(sides[0]) for b in range(sides[1]) if (a, b) != (0, 0)]
    return sorted(offsets, key=lambda o: -min(o[0], sides[0] - o[0]) - min(o[1], sides[1] - o[1]))


DP_OFF, HEAD_OFF = far_first((SIDE, SIDE)), far_first((DEEP, 2))

A1, F1 = lambda u: u, lambda u: 2 + u
A2, F2 = lambda u, m: 4 + u * 4 + m, lambda u, m: 12 + u * 4 + m
MATE = lambda a, b: 20 + a * 4 + b
ZED = 36
GATHER = 42
WHOLE, HALF, MATES, BESIDES = range(4)
PLANE, BESIDE = 176, 80
SHIFT = (0, 3, 1, 2)


def nt(a, b):
    return lax.dot_general(a, b, (((1,), (1,)), ((), ())), preferred_element_type=F32)


def nn(a, b):
    return jnp.dot(a, b, preferred_element_type=F32)


def kernel(student_hbm, teacher_hbm, mask_hbm, proto, patch_out, proto_out, loss_out,
           student, teacher, mask, loss, oh, su, tu, invn, nrm, nown, colinv, E, G, ET, suT, PG,
           U, PU, cr, zs, zr, csum, ysum, xr, yr, cs, racc, eacc, sscol,
           hsrc, hr, iva, ssa, agb, a2s, a2r, wide_out, dhi, dlo, ldr, lhr,
           psend, precv, gsend, grecv, lsem, osem):
    i, j = lax.axis_index("dp"), lax.axis_index("head")
    x, y = i // SIDE, lax.rem(i, SIDE)
    z, c = j // 2, lax.rem(j, 2)
    mate = (i, z * 2 + 1 - c)

    def proto_copy(k):
        cols = pl.ds(k * CW, CW)
        return pltpu.make_async_copy(proto.at[:, cols], nrm.at[:, cols], lsem.at[k])

    def patch_copy(k):
        return pltpu.make_async_copy((teacher_hbm, student_hbm)[k], (teacher, student)[k], lsem.at[CH + k])

    mask_copy = pltpu.make_async_copy(mask_hbm, mask, lsem.at[CH + 2])

    barrier = pltpu.get_barrier_semaphore()
    mask_copy.start()
    for k in (0, 1):
        patch_copy(k).start()
    for k in range(CH):
        proto_copy(k).start()
    for d in range(1, DP):
        pl.semaphore_signal(barrier, inc=1, device_id=(lax.rem(i + d, DP), j), device_id_type=MESH)
        pl.semaphore_signal(barrier, inc=1, device_id=(i, lax.rem(j + d, HEAD)), device_id_type=MESH)

    def send(src, dst, ph, dev, leave=None):
        leave = ph if leave is None else leave
        pltpu.make_async_remote_copy(src, dst, psend.at[leave], precv.at[ph], device_id=dev, device_id_type=MESH).start()

    def landed(like, ph):
        pltpu.make_async_copy(like, like, precv.at[ph]).wait()

    def sent(like, ph):
        pltpu.make_async_copy(like, like, psend.at[ph]).wait()

    def to_dp(src, dst, ph):
        for a, b in DP_OFF:
            send(src, dst, ph, (lax.rem(x + a, SIDE) * SIDE + lax.rem(y + b, SIDE), j))

    def to_head(src, dst, ph):
        for e, (a, b) in enumerate(HEAD_OFF):
            send(src, dst(e), ph, (i, lax.rem(z + a, DEEP) * 2 + lax.rem(c + b, 2)))

    def along_z(d):
        return (i, lax.rem(z + d, DEEP) * 2 + c)

    p = x * (1 - c) + y * c
    q = y * (1 - c) + x * c

    def at(dp_, dq_):
        pp, qq = lax.rem(p + dp_, SIDE), lax.rem(q + dq_, SIDE)
        return (pp * SIDE + qq) * (1 - c) + (qq * SIDE + pp) * c

    def first_axis(d):
        return (at(0, d), j)

    def second_axis(d):
        return (at(d, 0), j)

    odd = lax.rem(z, 2)

    def part(blk, u, half=None):
        first = odd * BESIDE + (0 if half is None else half * (PLANE // 2))
        rows = pl.ds(pl.multiple_of(first, 8), PLANE if half is None else PLANE // 2)
        return G.at[blk, c, u, rows]

    def beside(blk, which, s):
        first = which * PLANE + s * (BESIDE // 2)
        return G.at[blk, c, :, pl.ds(pl.multiple_of(first, 8), BESIDE // 2)]

    def gcopy(ref, kind, sid, dev):
        pltpu.make_async_remote_copy(ref, ref, gsend.at[kind], grecv.at[sid], device_id=dev, device_id_type=MESH).start()

    def gwait(like, sid):
        pltpu.make_async_copy(like, like, grecv.at[sid]).wait()

    both = G.at[0, c, :, pl.ds(0, PLANE)]
    both_halves = G.at[0, c, :, pl.ds(0, PLANE // 2)]

    def z_send(pairs, batch):
        for a, b in pairs:
            for s in (0, 1):
                gcopy(beside(at(a, b), odd, s), BESIDES, ZED + batch, along_z(1 if s == 0 else DEEP - 1))

    def n1(s):
        return (at(1 if s == 0 else 3, 0), j)

    def n2(s):
        return (at(0, 1 if s == 0 else 3), j)

    def a1_send(u):
        for s in (0, 1):
            gcopy(part(at(0, 0), u), WHOLE, A1(u), n1(s))

    def a1_wait(u):
        gwait(both, A1(u))

    def f1_send(u):
        for s in (0, 1):
            gcopy(part(at(3 if s == 0 else 1, 0), u, s), HALF, F1(u), n1(s))

    def f1_wait(u):
        gwait(both_halves, F1(u))

    def a2_send(u, m):
        for s in (0, 1):
            gcopy(part(at(SHIFT[m], 0), u), WHOLE, A2(u, m), n2(s))

    def a2_wait(u, m):
        gwait(both, A2(u, m))

    def f2_send(u, m):
        for s in (0, 1):
            gcopy(part(at(SHIFT[m], 3 if s == 0 else 1), u, s), HALF, F2(u, m), n2(s))

    def f2_wait(u, m):
        gwait(both_halves, F2(u, m))

    def mate_send(pairs, batch):
        gwait(G.at[pl.ds(0, len(pairs)), c, :, pl.ds(0, BESIDE)], ZED + batch)
        for a, b in pairs:
            gcopy(G.at[at(a, b), c], MATES, MATE(a, b), mate)

    def mate_wait(a, b):
        gwait(G.at[0, c], MATE(b, a))

    NEAR = ((1, 0), (3, 0), (0, 1), (0, 3))
    MID, MID_B = ((2, 0), (0, 2)), ((3, 1), (3, 3))
    FAR = ((3, 2), (1, 1), (1, 3))
    LAST = ((2, 1), (2, 3), (1, 2))
    END = ((2, 2),)
    READY_MID, READY_MID_B = ((2, 0), (0, 2)), ((3, 3),)
    READY_FAR = ((3, 1), (1, 1), (1, 3))
    READY_LAST = ((2, 3), (3, 2), (1, 2), (2, 1))

    def slot(n):
        if n == 0:
            a1_send(0)
            a2_send(0, 0)
            a2_send(1, 0)
        elif n == 1:
            a1_send(1)
        elif n == 2:
            a1_wait(0)
            f1_send(0)
            a2_send(0, 1)
            a2_wait(0, 0)
            f2_send(0, 0)
            a2_send(0, 2)
        elif n == 3:
            a2_send(1, 1)
            a2_send(1, 2)
            f1_wait(0)
            a2_send(0, 3)
            a2_wait(0, 1)
            f2_send(0, 1)
        elif n == 4:
            f1_wait(1)
            a2_send(1, 3)
            a2_wait(0, 2)
            f2_send(0, 2)
            f2_wait(0, 0)
            f2_wait(1, 0)
            z_send(MID, 1)
        elif n == 5:
            for u, m in ((1, 1), (1, 2), (0, 3)):
                a2_wait(u, m)
                f2_send(u, m)
            z_send(MID_B, 2)
        elif n == 6:
            a2_wait(1, 3)
            f2_send(1, 3)
            f2_wait(0, 2)
            f2_wait(1, 2)
            z_send(LAST, 4)
            mate_send(MID_B, 2)
        elif n == 7:
            f2_wait(0, 3)
            f2_wait(1, 3)
            z_send(END, 5)
        elif n == 8:
            mate_send(LAST, 4)

    def later_slot(n):
        if n == 2:
            a1_wait(1)
            f1_send(1)
            a2_wait(1, 0)
            f2_send(1, 0)
            z_send(NEAR, 0)
        elif n == 4:
            mate_send(NEAR, 0)
        elif n == 5:
            f2_wait(0, 1)
            f2_wait(1, 1)
            z_send(FAR, 3)
            mate_send(MID, 1)
        elif n == 7:
            mate_send(FAR, 3)
        elif n == 8:
            mate_send(END, 5)

    mask_copy.wait()

    @pl.loop(0, 8)
    def _(k):
        rows = pl.ds(pl.multiple_of(k * 128, 128), 128)
        patch = lax.broadcasted_iota(jnp.int32, (128, R), 0) + k * 128
        oh[rows, :] = jnp.where(patch == mask[...], 1.0, 0.0).astype(BF16)

    def unit(patches):
        rows = lax.dot_general(oh[...], patches[...], (((0,), (0,)), ((), ())), preferred_element_type=F32)
        inverse = lax.rsqrt(jnp.sum(rows * rows, axis=1, keepdims=True) + EPS)
        return (rows * inverse).astype(BF16), inverse

    patch_copy(0).wait()
    unit_t, _ = unit(teacher)
    tu[...] = unit_t
    patch_copy(1).wait()
    unit_s, inv_s = unit(student)
    su[...] = unit_s
    invn[...] = jnp.broadcast_to(inv_s, (R, 128))
    for half in (0, 1):
        rows = slice(half * (R // 2), (half + 1) * (R // 2))
        G[i, half, 0] = su[rows, :].astype(F32)
        G[i, half, 1] = tu[rows, :].astype(F32)

    def x_send(it, k):
        for d in (2, 1, 3):
            send(csum.at[it, k], xr.at[it, k, d - 1], X0 + it * CH + k, first_axis(d), XS)

    for k in range(CH):
        proto_copy(k).wait()

        for n in range(CW // W):
            cols = slice(k * CW + n * W, k * CW + (n + 1) * W)
            w = nrm[:, cols].astype(F32)
            inverse = lax.rsqrt(jnp.sum(w * w, axis=0, keepdims=True) + EPS)
            unit_cols = (w * inverse).astype(BF16)
            colinv[:, cols] = inverse
            nrm[:, cols] = unit_cols
            e = jnp.exp2(nn(tu[...], unit_cols) * TEACHER)
            E[:, cols] = e
            csum[0, k, :, n * W:(n + 1) * W] = jnp.sum(e, axis=0, keepdims=True)

        if k == 2:
            pl.semaphore_wait(barrier, DP + HEAD - 2)
            for n in range(3):
                x_send(0, n)
    x_send(0, 3)

    mine = pl.ds(pl.multiple_of(i * W, W), W)
    nown[...] = nrm[:, mine]
    PU[...] = jnp.zeros_like(PU)
    U[...] = jnp.zeros_like(U)
    PG[...] = jnp.zeros_like(PG)
    eacc[...] = jnp.zeros_like(eacc)

    def tiles(v):
        total = v[:, 0:128]
        for t in range(1, v.shape[1] // 128):
            total = total + v[:, t * 128:(t + 1) * 128]
        return total

    def student_chunks(first, last):
        @pl.loop(first // 4, last // 4)
        def _(k):
            for n in range(4):
                cols = pl.ds(pl.multiple_of(k * 4 * W + n * W, W), W)
                unit_cols = nrm[:, cols]
                e = jnp.exp2(nn(su[...], unit_cols) * STUDENT)
                eacc[...] += tiles(e)
                PU[...] += nt(e.astype(BF16), unit_cols).reshape(DEEP, 2, S, B)

    def across(v):
        return jnp.sum(v.T, axis=0, keepdims=True)

    def down(v):
        return jnp.broadcast_to(v, (128, R)).T

    def y_step(it, k):
        landed(xr.at[it, k], X0 + it * CH + k)
        ysum[it, k] = csum[it, k] + xr[it, k, 0] + xr[it, k, 1] + xr[it, k, 2]
        for d in (2, 1, 3):
            send(ysum.at[it, k], yr.at[it, k, d - 1], Y0 + it * CH + k, second_axis(d), YS)

    def row_step(it, k):
        landed(yr.at[it, k], Y0 + it * CH + k)
        cs[:, k * CW:(k + 1) * CW] = 1.0 / (K * (ysum[it, k] + yr[it, k, 0] + yr[it, k, 1] + yr[it, k, 2]))
        if it < ITERS - 1:
            @pl.loop(0, R // 64)
            def _(n):
                rows = pl.ds(pl.multiple_of(n * 64, 64), 64)
                total = jnp.zeros((64, 128), F32) if k == 0 else racc[rows, :]
                for t in range(k * CW // 128, (k + 1) * CW // 128):
                    total = total + E[rows, t * 128:(t + 1) * 128] * cs[:, t * 128:(t + 1) * 128]
                racc[rows, :] = total

    def last_pass():
        racc[...] = jnp.zeros_like(racc)

        @pl.loop(0, 2)
        def _(k):
            for n in range(4):
                cols = pl.ds(pl.multiple_of(k * (C // 2) + n * LAST_W, LAST_W), LAST_W)
                t = E[:, cols] * cs[:, cols]
                racc[...] += tiles(t)
                U[...] += nt(t.astype(BF16), nrm[:, cols]).reshape(DEEP, 2, S, B)

    def col_step(it, k):
        @pl.loop(0, CW // 1024)
        def _(n):
            part = pl.ds(pl.multiple_of(n * 1024, 1024), 1024)
            cols = pl.ds(pl.multiple_of(k * CW + n * 1024, 1024), 1024)
            total = jnp.zeros((8, 1024), F32)
            for r in range(R // 8):
                scale = sscol[r * 8:(r + 1) * 8, :]
                total = total + E[r * 8:(r + 1) * 8, cols] * jnp.concatenate([scale] * 8, axis=1)
            csum[it, k, :, part] = jnp.sum(total, axis=0, keepdims=True)

    def block(a, b):
        blk = at(a, b)
        s = G[blk, :, 0].reshape(R, B).astype(BF16)
        t = G[blk, :, 1].reshape(R, B).astype(BF16)
        rows = pl.ds(pl.multiple_of(blk * R, R), R)
        ET[rows, :] = jnp.exp2(nn(t, nown[...]) * TEACHER).astype(BF16)
        e = jnp.exp2(nn(s, nown[...]) * STUDENT).astype(BF16)
        turned = s.astype(F32).T
        suT[:, rows] = turned.astype(BF16)
        PG[...] += nn((turned * iva[blk]).astype(BF16), e)

    def blocks(pairs):
        for a, b in pairs:
            if (a, b) != (0, 0):
                mate_wait(a, b)
            block(a, b)

    def core_sum_send(v, which, ph):
        send(v.at[:, 1 - c], cr.at[which], ph, mate)

    def core_sum_wait(v, which, ph, zph):
        landed(cr.at[which], ph)
        zs[which] = v[:, c] + cr[which]
        for d in range(1, DEEP):
            send(zs.at[which, lax.rem(z + d, DEEP)], zr.at[which, d - 1], zph, along_z(d))

    def z_sum(which, zph):
        landed(zr.at[which], zph)
        total = zs[which, z]
        for d in range(DEEP - 1):
            total = total + zr[which, d]
        return total

    for it in range(ITERS):
        slot(3 * it)
        if it == 0:
            student_chunks(0, 8)
        elif it == 1:
            core_sum_wait(PU, 0, CP, ZP)
        elif it == 2:
            blocks(READY_MID)
        for k in range(CH):
            y_step(it, k)
        slot(3 * it + 1)
        if it == 0:
            student_chunks(8, 16)
        elif it == 1:
            landed(iva.at[pl.ds(0, DP - 1)], INV)
            blocks(((0, 0),))
            later_slot(4)
        elif it == 2:
            blocks(READY_MID_B)
            later_slot(7)
        for k in range(CH):
            row_step(it, k)
        if it == ITERS - 1:
            last_pass()
            core_sum_send(U, 1, CU)
        hsrc[it, :, 0:R] = across(racc[...])
        if it == 0:
            hsrc[it, :, R:2 * R] = across(eacc[...])
        wide = 2 * R if it == 0 else R
        to_head(hsrc.at[it, :, pl.ds(0, wide)], lambda e: hr.at[it, e, :, pl.ds(0, wide)], H0 + it)
        slot(3 * it + 2)
        if it == 0:
            core_sum_send(PU, 0, CP)
            later_slot(2)
        elif it == 1:
            blocks(NEAR)
            later_slot(5)
        elif it == 2:
            core_sum_wait(U, 1, CU, ZU)
            blocks(READY_FAR)
            later_slot(8)
        landed(hr.at[it, :, :, pl.ds(0, wide)], H0 + it)
        row_total = hsrc[it, :, 0:R]
        for d in range(HEAD - 1):
            row_total = row_total + hr[it, d, :, 0:R]
        if it == 0:
            exp_total = hsrc[it, :, R:2 * R]
            for d in range(HEAD - 1):
                exp_total = exp_total + hr[it, d, :, R:2 * R]
            iva[i] = 1.0 / exp_total
        if it < ITERS - 1:
            sscol[...] = down(1.0 / (ROWS * row_total))
            for k in range(CH):
                col_step(it + 1, k)
                x_send(it + 1, k)
        if it == 0:
            to_dp(iva.at[i], iva.at[i], INV)

    ssa[i] = 1.0 / row_total
    to_dp(ssa.at[i], ssa.at[i], SS)
    blocks(READY_LAST + END)

    target_sum = z_sum(1, ZU)
    student_sum = z_sum(0, ZP)
    own = lax.broadcasted_iota(jnp.int32, (S, R), 1) == lax.broadcasted_iota(jnp.int32, (S, R), 0) + j * S

    def pick(v):
        return jnp.sum(jnp.where(own, v, 0.0), axis=1, keepdims=True)

    own_rows = pl.ds(pl.multiple_of(j * S, S), S)
    in_half = pl.ds(pl.multiple_of(lax.rem(j, 8) * S, S), S)
    unit_rows = G[i, j // 8, 0, in_half]
    target_mean = target_sum * pick(ssa[i])
    exp_inv = pick(iva[i])
    unit_grad = GRAD * (student_sum * exp_inv - target_mean)
    row_dot = jnp.sum(unit_rows * unit_grad, axis=1, keepdims=True)
    agb[c, z] = invn[own_rows, 0:1] * (unit_grad - unit_rows * row_dot)
    for d in (4, 3, 5, 2, 6, 1, 7):
        send(agb.at[c, z], agb.at[c, z], AGZ, along_z(d))
    raw_mean = jnp.sum(unit_rows * target_mean, axis=1, keepdims=True)
    part_loss = jnp.sum(raw_mean * 10.0 + jnp.log(exp_inv), axis=0, keepdims=True)
    ldr[i] = jnp.broadcast_to(part_loss, (1, 128))
    to_dp(ldr.at[i], ldr.at[i], LD)

    landed(ssa.at[pl.ds(0, DP - 1)], SS)
    for k in range(4):
        rows = slice(k * 4 * R, (k + 1) * 4 * R)
        scale = jnp.concatenate([ssa[k * 4 + n] for n in range(4)], axis=1)
        suT[:, rows] = (suT[:, rows].astype(F32) * scale).astype(BF16)

    @pl.loop(0, 2)
    def _(h):
        half = pl.ds(pl.multiple_of(h * (W // 2), W // 2), W // 2)
        mine_half = pl.ds(pl.multiple_of(i * W + h * (W // 2), W // 2), W // 2)
        grad = jnp.zeros((B, W // 2), F32)
        for k in range(4):
            rows = slice(k * 4 * R, (k + 1) * 4 * R)
            grad = grad + nn(suT[:, rows], ET[rows, half])
        unit_cols = nown[:, half].astype(F32)
        normed_grad = GRAD * (PG[:, half] - cs[:, mine_half] * grad)
        col_dot = jnp.sum(unit_cols * normed_grad, axis=0, keepdims=True)
        a2s[h] = (colinv[:, mine_half] * (normed_grad - unit_cols * col_dot)).reshape(DP, B // DP, W // 2)
        for a, b in DP_OFF:
            to = lax.rem(x + a, SIDE) * SIDE + lax.rem(y + b, SIDE)
            send(a2s.at[h, to], a2r.at[h, i], A2A + h, (to, j))
        a2r[h, i] = a2s[h, i]

    landed(ldr.at[pl.ds(0, DP - 1)], LD)
    total = ldr[0]
    for d in range(1, DP):
        total = total + ldr[d]
    lhr[j] = total
    to_head(lhr.at[j], lambda e: lhr.at[j], LH)
    landed(agb.at[c, pl.ds(0, DEEP - 1)], AGZ)
    send(agb.at[c], agb.at[c], AGC, mate)

    def rows_in(h):
        for k in range(DEEP):
            v = agb[h, k]
            high = v.astype(BF16)
            dhi[k, h] = high
            dlo[k, h] = (v - high.astype(F32)).astype(BF16)

    rows_in(c)
    landed(agb.at[1 - c], AGC)
    rows_in(1 - c)
    outs = []
    for n in range(4):
        rows = slice(n * 256, (n + 1) * 256)
        patch = nn(oh[rows, :], dhi[...].reshape(R, B)) + nn(oh[rows, :], dlo[...].reshape(R, B))
        E[0:256, n * 256:(n + 1) * 256] = patch
        outs.append(pltpu.make_async_copy(E.at[pl.ds(0, 256), pl.ds(n * 256, 256)], patch_out.at[pl.ds(n * 256, 256)], osem.at[n]))
        outs[-1].start()
    landed(lhr.at[pl.ds(0, HEAD - 1)], LH)
    total = lhr[0]
    for d in range(1, HEAD):
        total = total + lhr[d]
    loss[...] = total * (-1.0 / ROWS)
    outs.append(pltpu.make_async_copy(loss, loss_out, osem.at[5]))
    outs[-1].start()

    sent(xr, XS)
    sent(yr, YS)
    for it in range(ITERS):
        wide = 2 * R if it == 0 else R
        sent(hr.at[it, :, :, pl.ds(0, wide)], H0 + it)
    sent(iva.at[pl.ds(0, DP - 1)], INV)
    sent(ssa.at[pl.ds(0, DP - 1)], SS)
    sent(cr.at[1], CU)
    sent(cr.at[0], CP)
    sent(zr.at[1], ZU)
    sent(zr.at[0], ZP)
    sent(agb.at[c, pl.ds(0, DEEP - 1)], AGZ)
    sent(agb.at[c], AGC)
    sent(ldr.at[pl.ds(0, DP - 1)], LD)
    sent(lhr.at[pl.ds(0, HEAD - 1)], LH)

    def gsent(like, kind):
        pltpu.make_async_copy(like, like, gsend.at[kind]).wait()

    gsent(G.at[pl.ds(0, 10), c, :, pl.ds(0, PLANE)], WHOLE)
    gsent(G.at[pl.ds(0, 10), c, :, pl.ds(0, PLANE // 2)], HALF)
    gsent(G.at[pl.ds(0, DP - 1), c], MATES)
    gsent(G.at[pl.ds(0, DP - 1), c, :, pl.ds(0, BESIDE)], BESIDES)

    for h in (0, 1):
        landed(a2r.at[h, pl.ds(0, DP - 1)], A2A + h)
        for d in range(DP):
            wide_out[:, d * W + h * W // 2:d * W + (h + 1) * W // 2] = a2r[h, d]
    outs.append(pltpu.make_async_copy(wide_out, proto_out, osem.at[4]))
    outs[-1].start()
    for h in (0, 1):
        sent(a2r.at[h, pl.ds(0, DP - 1)], A2A + h)
    for copy in outs:
        copy.wait()


def finish(patches, protos, patch_out, proto_out, patch_buf, proto_buf, isem, osem):
    parts = []
    for source, buf, target, count in ((patches, patch_buf, patch_out, 4), (protos, proto_buf, proto_out, 2)):
        size = source.shape[0] // count
        for n in range(count):
            rows, at = pl.ds(n * size, size), len(parts)
            parts.append((
                pltpu.make_async_copy(source.at[rows], buf.at[rows], isem.at[at]),
                pltpu.make_async_copy(buf.at[rows], target.at[rows], osem.at[at]),
            ))
    for get, _ in parts:
        get.start()
    for get, put in parts:
        get.wait()
        put.start()
    for _, put in parts:
        put.wait()


def on_device(student_patches, teacher_patches, mask_rows, prototypes):
    vm = pltpu.VMEM
    anywhere = pl.BlockSpec(memory_space=pl.ANY)
    results = (
        jax.ShapeDtypeStruct(student_patches.shape, F32),
        jax.ShapeDtypeStruct((B // DP, C), F32),
    )
    patches, protos, loss = pl.pallas_call(
        kernel,
        out_shape=results + (jax.ShapeDtypeStruct((1, 128), F32),),
        in_specs=[anywhere] * 4,
        out_specs=(anywhere,) * 3,
        scratch_shapes=[
            vm(student_patches.shape, BF16),
            vm(student_patches.shape, BF16),
            vm((1, R), jnp.int32),
            vm((1, 128), F32),
            vm((1024, R), BF16),
            vm((R, B), BF16),
            vm((R, B), BF16),
            vm((R, 128), F32),
            vm((B, C), BF16),
            vm((B, W), BF16),
            vm((1, C), F32),
            vm((R, C), F32),
            vm((DP, 2, 2, R // 2, B), F32),
            vm((DP * R, W), BF16),
            vm((B, DP * R), BF16),
            vm((B, W), F32),
            vm((DEEP, 2, S, B), F32),
            vm((DEEP, 2, S, B), F32),
            vm((2, DEEP, S, B), F32),
            vm((2, DEEP, S, B), F32),
            vm((2, DEEP - 1, S, B), F32),
            vm((ITERS, CH, 1, CW), F32),
            vm((ITERS, CH, 1, CW), F32),
            vm((ITERS, CH, SIDE - 1, 1, CW), F32),
            vm((ITERS, CH, SIDE - 1, 1, CW), F32),
            vm((1, C), F32),
            vm((R, 128), F32),
            vm((R, 128), F32),
            vm((R, 128), F32),
            vm((ITERS, 1, 2 * R), F32),
            vm((ITERS, HEAD - 1, 1, 2 * R), F32),
            vm((DP, 1, R), F32),
            vm((DP, 1, R), F32),
            vm((2, DEEP, S, B), F32),
            vm((2, DP, B // DP, W // 2), F32),
            vm((2, DP, B // DP, W // 2), F32),
            vm((B // DP, C), F32),
            vm((DEEP, 2, S, B), BF16),
            vm((DEEP, 2, S, B), BF16),
            vm((DP, 1, 128), F32),
            vm((HEAD, 1, 128), F32),
            pltpu.SemaphoreType.DMA((SMALL,)),
            pltpu.SemaphoreType.DMA((SMALL,)),
            pltpu.SemaphoreType.DMA((4,)),
            pltpu.SemaphoreType.DMA((GATHER,)),
            pltpu.SemaphoreType.DMA((CH + 3,)),
            pltpu.SemaphoreType.DMA((6,)),
        ],
        compiler_params=pltpu.CompilerParams(
            collective_id=0, has_side_effects=True, vmem_limit_bytes=63 * 2**20
        ),
    )(student_patches, teacher_patches, mask_rows.reshape(1, R), prototypes)
    patches, protos = pl.pallas_call(
        finish,
        out_shape=results,
        in_specs=[anywhere] * 2,
        out_specs=(anywhere, anywhere),
        scratch_shapes=[
            vm(student_patches.shape, F32),
            vm((B // DP, C), F32),
            pltpu.SemaphoreType.DMA((6,)),
            pltpu.SemaphoreType.DMA((6,)),
        ],
    )(patches, protos)
    return patches, protos, loss[0, 0]


def solution(mesh):
    return jax.shard_map(
        on_device,
        mesh=mesh,
        in_specs=(P("dp", None), P("dp", None), P("dp"), P(None, "head")),
        out_specs=(P("dp", None), P("dp", "head"), P()),
        check_vma=False,
    )
```

```python
import functools
import math

import jax
import jax.numpy as jnp
from jax import lax
from jax.experimental import pallas as pl
from jax.experimental.pallas import tpu as pltpu
from jax.sharding import PartitionSpec as P

MESH = pl.DeviceIdType.MESH
F32, BF16 = jnp.float32, jnp.bfloat16

EPS = 1e-06
LOG2E = math.log2(math.e)
TEACHER = 25.0 * LOG2E
STUDENT = 10.0 * LOG2E
GRAD = 4096.0 / 0.1
ITERS = 3
DP, HEAD, SIDE, DEEP = 16, 16, 4, 8
R, B, C = 512, 256, 8192
W = C // DP
ROWS, K = R * DP, C * HEAD
S = R // HEAD

CH = 4
CW = C // CH
LAST_W = 1024
X0, Y0, H0 = 0, ITERS * CH, 2 * ITERS * CH
INV, SS, CU, ZU, CP, ZP, AGZ, AGC, LD, LH, A2A = range(H0 + ITERS, H0 + ITERS + 11)
SMALL = A2A + 2
XS, YS = X0, Y0


def far_first(sides):
    offsets = [(a, b) for a in range(sides[0]) for b in range(sides[1]) if (a, b) != (0, 0)]
    return sorted(offsets, key=lambda o: -min(o[0], sides[0] - o[0]) - min(o[1], sides[1] - o[1]))


DP_OFF, HEAD_OFF = far_first((SIDE, SIDE)), far_first((DEEP, 2))

A1, F1 = lambda u: u, lambda u: 2 + u
A2, F2 = lambda u, m: 4 + u * 4 + m, lambda u, m: 12 + u * 4 + m
MATE = lambda a, b: 20 + a * 4 + b
ZED = 36
GATHER = 42
WHOLE, HALF, MATES, BESIDES = range(4)
PLANE, BESIDE = 176, 80
SHIFT = (0, 3, 1, 2)


def nt(a, b):
    return lax.dot_general(a, b, (((1,), (1,)), ((), ())), preferred_element_type=F32)


def nn(a, b):
    return jnp.dot(a, b, preferred_element_type=F32)


def kernel(student_hbm, teacher_hbm, mask_hbm, proto, patch_out, proto_out, loss_out,
           student, teacher, mask, loss, oh, su, tu, invn, nrm, nown, colinv, E, G, ET, suT, PG,
           U, PU, cr, zs, zr, csum, ysum, xr, yr, cs, racc, eacc, sscol,
           hsrc, hr, iva, ssa, agb, a2s, a2r, wide_out, dhi, dlo, ldr, lhr,
           psend, precv, gsend, grecv, lsem, osem):
    i, j = lax.axis_index("dp"), lax.axis_index("head")
    x, y = i // SIDE, lax.rem(i, SIDE)
    z, c = j // 2, lax.rem(j, 2)
    mate = (i, z * 2 + 1 - c)

    def proto_copy(k):
        cols = pl.ds(k * CW, CW)
        return pltpu.make_async_copy(proto.at[:, cols], nrm.at[:, cols], lsem.at[k])

    def patch_copy(k):
        return pltpu.make_async_copy((teacher_hbm, student_hbm)[k], (teacher, student)[k], lsem.at[CH + k])

    mask_copy = pltpu.make_async_copy(mask_hbm, mask, lsem.at[CH + 2])

    barrier = pltpu.get_barrier_semaphore()
    mask_copy.start()
    for k in (0, 1):
        patch_copy(k).start()
    for k in range(CH):
        proto_copy(k).start()
    for d in range(1, DP):
        pl.semaphore_signal(barrier, inc=1, device_id=(lax.rem(i + d, DP), j), device_id_type=MESH)
        pl.semaphore_signal(barrier, inc=1, device_id=(i, lax.rem(j + d, HEAD)), device_id_type=MESH)

    def send(src, dst, ph, dev, leave=None):
        leave = ph if leave is None else leave
        pltpu.make_async_remote_copy(src, dst, psend.at[leave], precv.at[ph], device_id=dev, device_id_type=MESH).start()

    def landed(like, ph):
        pltpu.make_async_copy(like, like, precv.at[ph]).wait()

    def sent(like, ph):
        pltpu.make_async_copy(like, like, psend.at[ph]).wait()

    def to_dp(src, dst, ph):
        for a, b in DP_OFF:
            send(src, dst, ph, (lax.rem(x + a, SIDE) * SIDE + lax.rem(y + b, SIDE), j))

    def to_head(src, dst, ph):
        for e, (a, b) in enumerate(HEAD_OFF):
            send(src, dst(e), ph, (i, lax.rem(z + a, DEEP) * 2 + lax.rem(c + b, 2)))

    def along_z(d):
        return (i, lax.rem(z + d, DEEP) * 2 + c)

    p = x * (1 - c) + y * c
    q = y * (1 - c) + x * c

    def at(dp_, dq_):
        pp, qq = lax.rem(p + dp_, SIDE), lax.rem(q + dq_, SIDE)
        return (pp * SIDE + qq) * (1 - c) + (qq * SIDE + pp) * c

    def first_axis(d):
        return (at(0, d), j)

    def second_axis(d):
        return (at(d, 0), j)

    odd = lax.rem(z, 2)

    def part(blk, u, half=None):
        first = odd * BESIDE + (0 if half is None else half * (PLANE // 2))
        rows = pl.ds(pl.multiple_of(first, 8), PLANE if half is None else PLANE // 2)
        return G.at[blk, c, u, rows]

    def beside(blk, which, s):
        first = which * PLANE + s * (BESIDE // 2)
        return G.at[blk, c, :, pl.ds(pl.multiple_of(first, 8), BESIDE // 2)]

    def gcopy(ref, kind, sid, dev):
        pltpu.make_async_remote_copy(ref, ref, gsend.at[kind], grecv.at[sid], device_id=dev, device_id_type=MESH).start()

    def gwait(like, sid):
        pltpu.make_async_copy(like, like, grecv.at[sid]).wait()

    both = G.at[0, c, :, pl.ds(0, PLANE)]
    both_halves = G.at[0, c, :, pl.ds(0, PLANE // 2)]

    def z_send(pairs, batch):
        for a, b in pairs:
            for s in (0, 1):
                gcopy(beside(at(a, b), odd, s), BESIDES, ZED + batch, along_z(1 if s == 0 else DEEP - 1))

    def n1(s):
        return (at(1 if s == 0 else 3, 0), j)

    def n2(s):
        return (at(0, 1 if s == 0 else 3), j)

    def a1_send(u):
        for s in (0, 1):
            gcopy(part(at(0, 0), u), WHOLE, A1(u), n1(s))

    def a1_wait(u):
        gwait(both, A1(u))

    def f1_send(u):
        for s in (0, 1):
            gcopy(part(at(3 if s == 0 else 1, 0), u, s), HALF, F1(u), n1(s))

    def f1_wait(u):
        gwait(both_halves, F1(u))

    def a2_send(u, m):
        for s in (0, 1):
            gcopy(part(at(SHIFT[m], 0), u), WHOLE, A2(u, m), n2(s))

    def a2_wait(u, m):
        gwait(both, A2(u, m))

    def f2_send(u, m):
        for s in (0, 1):
            gcopy(part(at(SHIFT[m], 3 if s == 0 else 1), u, s), HALF, F2(u, m), n2(s))

    def f2_wait(u, m):
        gwait(both_halves, F2(u, m))

    def mate_send(pairs, batch):
        gwait(G.at[pl.ds(0, len(pairs)), c, :, pl.ds(0, BESIDE)], ZED + batch)
        for a, b in pairs:
            gcopy(G.at[at(a, b), c], MATES, MATE(a, b), mate)

    def mate_wait(a, b):
        gwait(G.at[0, c], MATE(b, a))

    NEAR = ((1, 0), (3, 0), (0, 1), (0, 3))
    MID, MID_B = ((2, 0), (0, 2)), ((3, 1), (3, 3))
    FAR = ((3, 2), (1, 1), (1, 3))
    LAST = ((2, 1), (2, 3), (1, 2))
    END = ((2, 2),)
    READY_MID, READY_MID_B = ((2, 0), (0, 2)), ((3, 3),)
    READY_FAR = ((3, 1), (1, 1), (1, 3))
    READY_LAST = ((2, 3), (3, 2), (1, 2), (2, 1))

    def slot(n):
        if n == 0:
            a1_send(0)
            a2_send(0, 0)
            a2_send(1, 0)
        elif n == 1:
            a1_send(1)
        elif n == 2:
            a1_wait(0)
            f1_send(0)
            a2_send(0, 1)
            a2_wait(0, 0)
            f2_send(0, 0)
            a2_send(0, 2)
        elif n == 3:
            a2_send(1, 1)
            a2_send(1, 2)
            f1_wait(0)
            a2_send(0, 3)
            a2_wait(0, 1)
            f2_send(0, 1)
        elif n == 4:
            f1_wait(1)
            a2_send(1, 3)
            a2_wait(0, 2)
            f2_send(0, 2)
            f2_wait(0, 0)
            f2_wait(1, 0)
            z_send(MID, 1)
        elif n == 5:
            for u, m in ((1, 1), (1, 2), (0, 3)):
                a2_wait(u, m)
                f2_send(u, m)
            z_send(MID_B, 2)
        elif n == 6:
            a2_wait(1, 3)
            f2_send(1, 3)
            f2_wait(0, 2)
            f2_wait(1, 2)
            z_send(LAST, 4)
            mate_send(MID_B, 2)
        elif n == 7:
            f2_wait(0, 3)
            f2_wait(1, 3)
            z_send(END, 5)

    def later_slot(n):
        if n == 2:
            a1_wait(1)
            f1_send(1)
            a2_wait(1, 0)
            f2_send(1, 0)
            z_send(NEAR, 0)
        elif n == 4:
            mate_send(NEAR, 0)
        elif n == 5:
            f2_wait(0, 1)
            f2_wait(1, 1)
            z_send(FAR, 3)
            mate_send(MID, 1)
        elif n == 7:
            mate_send(FAR, 3)
        elif n == 8:
            mate_send(LAST, 4)
        elif n == 9:
            mate_send(END, 5)

    mask_copy.wait()

    @pl.loop(0, 8)
    def _(k):
        rows = pl.ds(pl.multiple_of(k * 128, 128), 128)
        patch = lax.broadcasted_iota(jnp.int32, (128, R), 0) + k * 128
        oh[rows, :] = jnp.where(patch == mask[...], 1.0, 0.0).astype(BF16)

    def unit(patches):
        rows = lax.dot_general(oh[...], patches[...], (((0,), (0,)), ((), ())), preferred_element_type=F32)
        inverse = lax.rsqrt(jnp.sum(rows * rows, axis=1, keepdims=True) + EPS)
        return (rows * inverse).astype(BF16), inverse

    patch_copy(0).wait()
    unit_t, _ = unit(teacher)
    tu[...] = unit_t
    patch_copy(1).wait()
    unit_s, inv_s = unit(student)
    su[...] = unit_s
    invn[...] = jnp.broadcast_to(inv_s, (R, 128))
    for half in (0, 1):
        rows = slice(half * (R // 2), (half + 1) * (R // 2))
        G[i, half, 0] = su[rows, :].astype(F32)
        G[i, half, 1] = tu[rows, :].astype(F32)

    def x_send(it, k):
        for d in (2, 1, 3):
            send(csum.at[it, k], xr.at[it, k, d - 1], X0 + it * CH + k, first_axis(d), XS)

    for k in range(CH):
        proto_copy(k).wait()

        for n in range(CW // W):
            cols = slice(k * CW + n * W, k * CW + (n + 1) * W)
            w = nrm[:, cols].astype(F32)
            inverse = lax.rsqrt(jnp.sum(w * w, axis=0, keepdims=True) + EPS)
            unit_cols = (w * inverse).astype(BF16)
            colinv[:, cols] = inverse
            nrm[:, cols] = unit_cols
            e = jnp.exp2(nn(tu[...], unit_cols) * TEACHER)
            E[:, cols] = e
            csum[0, k, :, n * W:(n + 1) * W] = jnp.sum(e, axis=0, keepdims=True)

        if k == 2:
            pl.semaphore_wait(barrier, DP + HEAD - 2)
            for n in range(3):
                x_send(0, n)
    x_send(0, 3)

    mine = pl.ds(pl.multiple_of(i * W, W), W)
    nown[...] = nrm[:, mine]
    PU[...] = jnp.zeros_like(PU)
    U[...] = jnp.zeros_like(U)
    PG[...] = jnp.zeros_like(PG)
    eacc[...] = jnp.zeros_like(eacc)

    def tiles(v):
        total = v[:, 0:128]
        for t in range(1, v.shape[1] // 128):
            total = total + v[:, t * 128:(t + 1) * 128]
        return total

    def student_chunks(first, last):
        @pl.loop(first // 4, last // 4)
        def _(k):
            for n in range(4):
                cols = pl.ds(pl.multiple_of(k * 4 * W + n * W, W), W)
                unit_cols = nrm[:, cols]
                e = jnp.exp2(nn(su[...], unit_cols) * STUDENT)
                eacc[...] += tiles(e)
                PU[...] += nt(e.astype(BF16), unit_cols).reshape(DEEP, 2, S, B)

    def across(v):
        return jnp.sum(v.T, axis=0, keepdims=True)

    def down(v):
        return jnp.broadcast_to(v, (128, R)).T

    def y_step(it, k):
        landed(xr.at[it, k], X0 + it * CH + k)
        ysum[it, k] = csum[it, k] + xr[it, k, 0] + xr[it, k, 1] + xr[it, k, 2]
        for d in (2, 1, 3):
            send(ysum.at[it, k], yr.at[it, k, d - 1], Y0 + it * CH + k, second_axis(d), YS)

    def row_step(it, k):
        landed(yr.at[it, k], Y0 + it * CH + k)
        cs[:, k * CW:(k + 1) * CW] = 1.0 / (K * (ysum[it, k] + yr[it, k, 0] + yr[it, k, 1] + yr[it, k, 2]))
        if it < ITERS - 1:
            @pl.loop(0, R // 64)
            def _(n):
                rows = pl.ds(pl.multiple_of(n * 64, 64), 64)
                total = jnp.zeros((64, 128), F32) if k == 0 else racc[rows, :]
                for t in range(k * CW // 128, (k + 1) * CW // 128):
                    total = total + E[rows, t * 128:(t + 1) * 128] * cs[:, t * 128:(t + 1) * 128]
                racc[rows, :] = total

    def last_pass():
        racc[...] = jnp.zeros_like(racc)

        @pl.loop(0, 2)
        def _(k):
            for n in range(4):
                cols = pl.ds(pl.multiple_of(k * (C // 2) + n * LAST_W, LAST_W), LAST_W)
                t = E[:, cols] * cs[:, cols]
                racc[...] += tiles(t)
                U[...] += nt(t.astype(BF16), nrm[:, cols]).reshape(DEEP, 2, S, B)

    def col_step(it, k):
        @pl.loop(0, CW // 1024)
        def _(n):
            part = pl.ds(pl.multiple_of(n * 1024, 1024), 1024)
            cols = pl.ds(pl.multiple_of(k * CW + n * 1024, 1024), 1024)
            total = jnp.zeros((8, 1024), F32)
            for r in range(R // 8):
                scale = sscol[r * 8:(r + 1) * 8, :]
                total = total + E[r * 8:(r + 1) * 8, cols] * jnp.concatenate([scale] * 8, axis=1)
            csum[it, k, :, part] = jnp.sum(total, axis=0, keepdims=True)

    def block(a, b):
        blk = at(a, b)
        s = G[blk, :, 0].reshape(R, B).astype(BF16)
        t = G[blk, :, 1].reshape(R, B).astype(BF16)
        rows = pl.ds(pl.multiple_of(blk * R, R), R)
        ET[rows, :] = jnp.exp2(nn(t, nown[...]) * TEACHER).astype(BF16)
        e = jnp.exp2(nn(s, nown[...]) * STUDENT).astype(BF16)
        turned = s.astype(F32).T
        suT[:, rows] = turned.astype(BF16)
        PG[...] += nn((turned * iva[blk]).astype(BF16), e)

    def blocks(pairs):
        for a, b in pairs:
            if (a, b) != (0, 0):
                mate_wait(a, b)
            block(a, b)

    def core_sum_send(v, which, ph):
        send(v.at[:, 1 - c], cr.at[which], ph, mate)

    def core_sum_wait(v, which, ph, zph):
        landed(cr.at[which], ph)
        zs[which] = v[:, c] + cr[which]
        for d in range(1, DEEP):
            send(zs.at[which, lax.rem(z + d, DEEP)], zr.at[which, d - 1], zph, along_z(d))

    def z_sum(which, zph):
        landed(zr.at[which], zph)
        total = zs[which, z]
        for d in range(DEEP - 1):
            total = total + zr[which, d]
        return total

    for it in range(ITERS):
        slot(3 * it)
        if it == 0:
            student_chunks(0, 8)
        elif it == 1:
            core_sum_wait(PU, 0, CP, ZP)
        elif it == 2:
            blocks(READY_MID)
        for k in range(CH):
            y_step(it, k)
        slot(3 * it + 1)
        if it == 0:
            student_chunks(8, 16)
        elif it == 1:
            landed(iva.at[pl.ds(0, DP - 1)], INV)
            blocks(((0, 0),))
            later_slot(4)
        elif it == 2:
            blocks(READY_MID_B)
            later_slot(7)
        for k in range(CH):
            row_step(it, k)
        if it == ITERS - 1:
            last_pass()
            core_sum_send(U, 1, CU)
        hsrc[it, :, 0:R] = across(racc[...])
        if it == 0:
            hsrc[it, :, R:2 * R] = across(eacc[...])
        wide = 2 * R if it == 0 else R
        to_head(hsrc.at[it, :, pl.ds(0, wide)], lambda e: hr.at[it, e, :, pl.ds(0, wide)], H0 + it)
        slot(3 * it + 2)
        if it == 0:
            core_sum_send(PU, 0, CP)
            later_slot(2)
        elif it == 1:
            blocks(NEAR)
            later_slot(5)
        elif it == 2:
            core_sum_wait(U, 1, CU, ZU)
            blocks(READY_FAR)
            later_slot(8)
        landed(hr.at[it, :, :, pl.ds(0, wide)], H0 + it)
        row_total = hsrc[it, :, 0:R]
        for d in range(HEAD - 1):
            row_total = row_total + hr[it, d, :, 0:R]
        if it == 0:
            exp_total = hsrc[it, :, R:2 * R]
            for d in range(HEAD - 1):
                exp_total = exp_total + hr[it, d, :, R:2 * R]
            iva[i] = 1.0 / exp_total
        if it < ITERS - 1:
            sscol[...] = down(1.0 / (ROWS * row_total))
            for k in range(CH):
                col_step(it + 1, k)
                x_send(it + 1, k)
        if it == 0:
            to_dp(iva.at[i], iva.at[i], INV)

    ssa[i] = 1.0 / row_total
    to_dp(ssa.at[i], ssa.at[i], SS)
    later_slot(9)
    blocks(READY_LAST + END)

    target_sum = z_sum(1, ZU)
    student_sum = z_sum(0, ZP)
    own = lax.broadcasted_iota(jnp.int32, (S, R), 1) == lax.broadcasted_iota(jnp.int32, (S, R), 0) + j * S

    def pick(v):
        return jnp.sum(jnp.where(own, v, 0.0), axis=1, keepdims=True)

    own_rows = pl.ds(pl.multiple_of(j * S, S), S)
    in_half = pl.ds(pl.multiple_of(lax.rem(j, 8) * S, S), S)
    unit_rows = G[i, j // 8, 0, in_half]
    target_mean = target_sum * pick(ssa[i])
    exp_inv = pick(iva[i])
    unit_grad = GRAD * (student_sum * exp_inv - target_mean)
    row_dot = jnp.sum(unit_rows * unit_grad, axis=1, keepdims=True)
    agb[c, z] = invn[own_rows, 0:1] * (unit_grad - unit_rows * row_dot)
    for d in (4, 3, 5, 2, 6, 1, 7):
        send(agb.at[c, z], agb.at[c, z], AGZ, along_z(d))
    raw_mean = jnp.sum(unit_rows * target_mean, axis=1, keepdims=True)
    part_loss = jnp.sum(raw_mean * 10.0 + jnp.log(exp_inv), axis=0, keepdims=True)
    ldr[i] = jnp.broadcast_to(part_loss, (1, 128))
    to_dp(ldr.at[i], ldr.at[i], LD)

    landed(ssa.at[pl.ds(0, DP - 1)], SS)
    for k in range(4):
        rows = slice(k * 4 * R, (k + 1) * 4 * R)
        scale = jnp.concatenate([ssa[k * 4 + n] for n in range(4)], axis=1)
        suT[:, rows] = (suT[:, rows].astype(F32) * scale).astype(BF16)

    @pl.loop(0, 2)
    def _(h):
        half = pl.ds(pl.multiple_of(h * (W // 2), W // 2), W // 2)
        mine_half = pl.ds(pl.multiple_of(i * W + h * (W // 2), W // 2), W // 2)
        grad = jnp.zeros((B, W // 2), F32)
        for k in range(4):
            rows = slice(k * 4 * R, (k + 1) * 4 * R)
            grad = grad + nn(suT[:, rows], ET[rows, half])
        unit_cols = nown[:, half].astype(F32)
        normed_grad = GRAD * (PG[:, half] - cs[:, mine_half] * grad)
        col_dot = jnp.sum(unit_cols * normed_grad, axis=0, keepdims=True)
        a2s[h] = (colinv[:, mine_half] * (normed_grad - unit_cols * col_dot)).reshape(DP, B // DP, W // 2)
        for a, b in DP_OFF:
            to = lax.rem(x + a, SIDE) * SIDE + lax.rem(y + b, SIDE)
            send(a2s.at[h, to], a2r.at[h, i], A2A + h, (to, j))
        a2r[h, i] = a2s[h, i]

    landed(ldr.at[pl.ds(0, DP - 1)], LD)
    total = ldr[0]
    for d in range(1, DP):
        total = total + ldr[d]
    lhr[j] = total
    to_head(lhr.at[j], lambda e: lhr.at[j], LH)
    landed(agb.at[c, pl.ds(0, DEEP - 1)], AGZ)
    send(agb.at[c], agb.at[c], AGC, mate)

    def rows_in(h):
        for k in range(DEEP):
            v = agb[h, k]
            high = v.astype(BF16)
            dhi[k, h] = high
            dlo[k, h] = (v - high.astype(F32)).astype(BF16)

    rows_in(c)
    landed(agb.at[1 - c], AGC)
    rows_in(1 - c)
    outs = []
    for n in range(4):
        rows = slice(n * 256, (n + 1) * 256)
        patch = nn(oh[rows, :], dhi[...].reshape(R, B)) + nn(oh[rows, :], dlo[...].reshape(R, B))
        E[0:256, n * 256:(n + 1) * 256] = patch
        outs.append(pltpu.make_async_copy(E.at[pl.ds(0, 256), pl.ds(n * 256, 256)], patch_out.at[pl.ds(n * 256, 256)], osem.at[n]))
        outs[-1].start()
    landed(lhr.at[pl.ds(0, HEAD - 1)], LH)
    total = lhr[0]
    for d in range(1, HEAD):
        total = total + lhr[d]
    loss[...] = total * (-1.0 / ROWS)
    outs.append(pltpu.make_async_copy(loss, loss_out, osem.at[5]))
    outs[-1].start()

    sent(xr, XS)
    sent(yr, YS)
    for it in range(ITERS):
        wide = 2 * R if it == 0 else R
        sent(hr.at[it, :, :, pl.ds(0, wide)], H0 + it)
    sent(iva.at[pl.ds(0, DP - 1)], INV)
    sent(ssa.at[pl.ds(0, DP - 1)], SS)
    sent(cr.at[1], CU)
    sent(cr.at[0], CP)
    sent(zr.at[1], ZU)
    sent(zr.at[0], ZP)
    sent(agb.at[c, pl.ds(0, DEEP - 1)], AGZ)
    sent(agb.at[c], AGC)
    sent(ldr.at[pl.ds(0, DP - 1)], LD)
    sent(lhr.at[pl.ds(0, HEAD - 1)], LH)

    def gsent(like, kind):
        pltpu.make_async_copy(like, like, gsend.at[kind]).wait()

    gsent(G.at[pl.ds(0, 10), c, :, pl.ds(0, PLANE)], WHOLE)
    gsent(G.at[pl.ds(0, 10), c, :, pl.ds(0, PLANE // 2)], HALF)
    gsent(G.at[pl.ds(0, DP - 1), c], MATES)
    gsent(G.at[pl.ds(0, DP - 1), c, :, pl.ds(0, BESIDE)], BESIDES)

    for h in (0, 1):
        landed(a2r.at[h, pl.ds(0, DP - 1)], A2A + h)
        for d in range(DP):
            wide_out[:, d * W + h * W // 2:d * W + (h + 1) * W // 2] = a2r[h, d]
    outs.append(pltpu.make_async_copy(wide_out, proto_out, osem.at[4]))
    outs[-1].start()
    for h in (0, 1):
        sent(a2r.at[h, pl.ds(0, DP - 1)], A2A + h)
    for copy in outs:
        copy.wait()


def finish(patches, protos, patch_out, proto_out, patch_buf, proto_buf, isem, osem):
    parts = []
    for source, buf, target, count in ((patches, patch_buf, patch_out, 4), (protos, proto_buf, proto_out, 2)):
        size = source.shape[0] // count
        for n in range(count):
            rows, at = pl.ds(n * size, size), len(parts)
            parts.append((
                pltpu.make_async_copy(source.at[rows], buf.at[rows], isem.at[at]),
                pltpu.make_async_copy(buf.at[rows], target.at[rows], osem.at[at]),
            ))
    for get, _ in parts:
        get.start()
    for get, put in parts:
        get.wait()
        put.start()
    for _, put in parts:
        put.wait()


def on_device(student_patches, teacher_patches, mask_rows, prototypes):
    vm = pltpu.VMEM
    anywhere = pl.BlockSpec(memory_space=pl.ANY)
    results = (
        jax.ShapeDtypeStruct(student_patches.shape, F32),
        jax.ShapeDtypeStruct((B // DP, C), F32),
    )
    patches, protos, loss = pl.pallas_call(
        kernel,
        out_shape=results + (jax.ShapeDtypeStruct((1, 128), F32),),
        in_specs=[anywhere] * 4,
        out_specs=(anywhere,) * 3,
        scratch_shapes=[
            vm(student_patches.shape, BF16),
            vm(student_patches.shape, BF16),
            vm((1, R), jnp.int32),
            vm((1, 128), F32),
            vm((1024, R), BF16),
            vm((R, B), BF16),
            vm((R, B), BF16),
            vm((R, 128), F32),
            vm((B, C), BF16),
            vm((B, W), BF16),
            vm((1, C), F32),
            vm((R, C), F32),
            vm((DP, 2, 2, R // 2, B), F32),
            vm((DP * R, W), BF16),
            vm((B, DP * R), BF16),
            vm((B, W), F32),
            vm((DEEP, 2, S, B), F32),
            vm((DEEP, 2, S, B), F32),
            vm((2, DEEP, S, B), F32),
            vm((2, DEEP, S, B), F32),
            vm((2, DEEP - 1, S, B), F32),
            vm((ITERS, CH, 1, CW), F32),
            vm((ITERS, CH, 1, CW), F32),
            vm((ITERS, CH, SIDE - 1, 1, CW), F32),
            vm((ITERS, CH, SIDE - 1, 1, CW), F32),
            vm((1, C), F32),
            vm((R, 128), F32),
            vm((R, 128), F32),
            vm((R, 128), F32),
            vm((ITERS, 1, 2 * R), F32),
            vm((ITERS, HEAD - 1, 1, 2 * R), F32),
            vm((DP, 1, R), F32),
            vm((DP, 1, R), F32),
            vm((2, DEEP, S, B), F32),
            vm((2, DP, B // DP, W // 2), F32),
            vm((2, DP, B // DP, W // 2), F32),
            vm((B // DP, C), F32),
            vm((DEEP, 2, S, B), BF16),
            vm((DEEP, 2, S, B), BF16),
            vm((DP, 1, 128), F32),
            vm((HEAD, 1, 128), F32),
            pltpu.SemaphoreType.DMA((SMALL,)),
            pltpu.SemaphoreType.DMA((SMALL,)),
            pltpu.SemaphoreType.DMA((4,)),
            pltpu.SemaphoreType.DMA((GATHER,)),
            pltpu.SemaphoreType.DMA((CH + 3,)),
            pltpu.SemaphoreType.DMA((6,)),
        ],
        compiler_params=pltpu.CompilerParams(
            collective_id=0, has_side_effects=True, vmem_limit_bytes=63 * 2**20
        ),
    )(student_patches, teacher_patches, mask_rows.reshape(1, R), prototypes)
    patches, protos = pl.pallas_call(
        finish,
        out_shape=results,
        in_specs=[anywhere] * 2,
        out_specs=(anywhere, anywhere),
        scratch_shapes=[
            vm(student_patches.shape, F32),
            vm((B // DP, C), F32),
            pltpu.SemaphoreType.DMA((6,)),
            pltpu.SemaphoreType.DMA((6,)),
        ],
    )(patches, protos)
    return patches, protos, loss[0, 0]


def solution(mesh):
    return jax.shard_map(
        on_device,
        mesh=mesh,
        in_specs=(P("dp", None), P("dp", None), P("dp"), P(None, "head")),
        out_specs=(P("dp", None), P("dp", "head"), P()),
        check_vma=False,
    )
```
